128 devices in a mesh: lon: 32 (over y, z, core), lat: 4 (over x).
Axes of the slice: x: 4, y: 4, z: 4, core: 2. Of those that a mesh axis runs over, the one named last changes fastest.
Arguments:
- atmos_flux: float32 [32768, 6, 128], P(('lon', 'lat')), may hold values from -6 to 6
- remap_blocks: bfloat16 [32768, 128, 128], P(('lon', 'lat')), may hold values from -0.5 to 0.5
- row_owner: int32 [32768, 1], P(('lon', 'lat')), may hold values from 0 to 127; in each aligned block of 256 rows (0 to 255, 256 to 511, ...) at most 4 rows name the same one
- row_target: int32 [32768], P(('lon', 'lat')), may hold values from 0 to 31
- tracers: float32 [2, 8, 128, 4096], P(None, None, 'lat', 'lon'), may hold values from -6 to 6
- east_vel: float32 [8, 128, 4096], P(None, 'lat', 'lon'), may hold values from -0.2 to 0.2
- north_vel: float32 [8, 128, 4096], P(None, 'lat', 'lon'), may hold values from -0.2 to 0.2
- mix_kappa: float32 [8, 128, 4096], P(None, 'lat', 'lon'), may hold values from 0.05 to 2
- levels: int32 [128, 4096], P('lat', 'lon'), may hold values from 0 to 8
Outputs:
- tracers_next: float32 [2, 8, 128, 4096], P(None, None, 'lat', 'lon')
- atmos_state: float32 [32768, 2, 128], P(('lon', 'lat'))
The draws below stay inside these ranges and needn't reach their ends.
Inputs may be any that keep to these rules, and one draw needn't show every extreme that they name: `row_owner`: in the rows of one device no ocean device is named more than 4 times, and some ocean device is named exactly 4 times.
All inputs are finite; a program needn't handle non-finite values.
Results may differ from the reference program's by a relative error of at most 0.0003.
Values sent between devices are 32-bit elements; how exact they have to be, the bound alone decides.
No kernel may reach another device: no remote copies, remote signals or barrier semaphores. Data moves between devices by JAX's collectives and lax.ppermute only.
A program may use at most 64 MiB of HBM per device.

```python
import math
import jax
import jax.numpy as jnp
import numpy as np
from jax import lax

ROWPTS = 128
NFLUX = 6
LEV = 8
CX = 128
CY = 32
AROWS = 256
CAP = 4
AIR_ROW_TOTAL = 32768
NX = 4096
NY = 128
N_LON = 32
N_LAT = 4
DEVICES = 128


def place_ends(entries, rng, low, high):
    longest = entries.shape.index(max(entries.shape))
    spots = []
    for shift in (0, 1):
        where = [jax.random.randint(jax.random.fold_in(rng, axis), (), 0, length) for axis, length in enumerate(entries.shape)]
        where[longest] = (where[longest] + shift) % entries.shape[longest]
        spots.append(tuple(where))
    return entries.at[spots[0]].set(low).at[spots[1]].set(high)


def block_levels(own_key, dims, split, low, largest):
    def one(axis_at, shards_of):
        steps = jax.random.uniform(jax.random.fold_in(jax.random.fold_in(own_key, 6), axis_at), (shards_of,), jnp.float32, low / len(split), largest / len(split))
        return jnp.repeat(jnp.exp(steps), dims[axis_at] // shards_of).reshape((-1,) + (1,) * (len(dims) - axis_at - 1))

    gain = one(*split[0])
    for cut in split[1:]:
        gain = gain * one(*cut)
    return gain


def deal_out(rng, own, number, rows, number_of, top, reach, lean):
    sequence = jax.random.permutation(rng, number_of)
    heavy_load, usual = portions_of(number_of, rows * top, reach, lean, True), portions_of(number_of, rows * top, reach, lean, False)
    places = jnp.arange(number_of)

    def named(tallies, offset_by):
        used = int((tallies > 0).sum())
        fixed = max(1, used // 4)
        shifted = fixed + (places - fixed + offset_by * (used - fixed)) % max(1, number_of - fixed)
        return jnp.zeros((number_of,), jnp.int32).at[sequence[jnp.where(places < fixed, places, shifted)]].set(jnp.asarray(tallies, jnp.int32))

    tallies = jnp.where(number % 4 == 0, named(heavy_load, number // 4), named(usual, number - number // 4 - 1))
    mixed = jax.random.permutation(jax.random.fold_in(own, 3), number_of)
    giver, sink = mixed[0:number_of // 2 * 2:2], mixed[1:number_of // 2 * 2:2]
    margin = jnp.minimum(tallies[giver] - 1, reach - tallies[sink]) // 2
    margin = jnp.where((giver == sequence[0]) | (sink == sequence[0]) | (tallies[sink] == 0), 0, jnp.maximum(margin, 0))
    shifted = jax.random.randint(jax.random.fold_in(own, 4), (number_of // 2,), 0, 1 << 20) % (margin + 1)
    tallies = tallies.at[giver].add(-shifted).at[sink].add(shifted)
    items = jnp.searchsorted(jnp.cumsum(tallies), jnp.arange(rows * top), side="right").astype(jnp.int32)
    listing = items.reshape(top, rows).T
    listing = listing[jax.random.permutation(jax.random.fold_in(own, 1), rows)]
    offset_by = jax.random.randint(jax.random.fold_in(own, 2), (rows, 1), 0, top)
    return jnp.take_along_axis(listing, (jnp.arange(top)[None, :] + offset_by) % top, axis=1)


def portions_of(count, total, reach, lean, full):
    weights = [(1 << 20) // math.isqrt(grade ** lean) + 1 for grade in range(1, count + 1)]
    largest = reach if full else min(reach, max(-(-total // count), total * weights[0] // sum(weights)))
    least = 1 if total - largest >= count - 1 else 0
    holding, spare = [largest] + [least] * (count - 1), total - largest - least * (count - 1)
    while spare > 0:
        candidates = [i for i in range(1, count) if holding[i] < largest] or [i for i in range(1, count) if holding[i] < reach]
        pool, left = sum([weights[i] for i in candidates]), spare
        for i in candidates:
            more = min(reach - holding[i], max(1, left * weights[i] // pool), spare)
            holding[i] = holding[i] + more
            spare = spare - more
    return np.array(holding)


def noise(key, shape, spread, limit, cuts=(), held_as=jnp.bfloat16):
    level = block_levels(key, shape, cuts, -0.22, 0.18) if cuts else 1.0
    result = jax.random.normal(key, shape, jnp.float32) * spread * level
    return jnp.minimum(jnp.maximum(result, -limit), limit).astype(held_as)


def setup_inputs(seed: int = 0) -> dict:
    streams_of = jax.random.split(jax.random.key(seed), 10)
    atmos_flux = noise(streams_of[0], (AIR_ROW_TOTAL, NFLUX, ROWPTS), 1.0, 6.0, ((0, 128),), jnp.float32)
    remap_blocks = noise(streams_of[1], (AIR_ROW_TOTAL, ROWPTS, CX), ROWPTS ** -0.5, 0.5, ((0, 128),))
    row_owner_keys = jax.random.split(jax.random.fold_in(streams_of[2], 1), AIR_ROW_TOTAL // AROWS)
    row_owner_turns = jax.random.permutation(jax.random.fold_in(streams_of[2], 3), AIR_ROW_TOTAL // AROWS)
    row_owner = jax.vmap(lambda own, number: deal_out(jax.random.fold_in(streams_of[2], 2), own, number, AROWS, DEVICES, 1, CAP, 2))(row_owner_keys, row_owner_turns).reshape((AIR_ROW_TOTAL, 1))
    row_target = place_ends(jax.random.randint(streams_of[3], (AIR_ROW_TOTAL,), 0, CY), jax.random.fold_in(streams_of[3], 1), 0, CY - 1).astype(jnp.int32)
    tracers = noise(streams_of[4], (2, LEV, NY, NX), 1.0, 6.0, ((2, 4), (3, 32)), jnp.float32)
    east_vel = jnp.clip(jax.random.uniform(streams_of[5], (LEV, NY, NX), jnp.float32, -0.2, 0.2) * block_levels(streams_of[5], (LEV, NY, NX), ((1, 4), (2, 32)), -0.4, 0.0), -0.2, 0.2)
    north_vel = jnp.clip(jax.random.uniform(streams_of[6], (LEV, NY, NX), jnp.float32, -0.2, 0.2) * block_levels(streams_of[6], (LEV, NY, NX), ((1, 4), (2, 32)), -0.4, 0.0), -0.2, 0.2)
    mix_kappa = jnp.clip(jnp.exp(math.log(2.0) - 3.6888794 * jax.random.uniform(streams_of[7], (LEV, NY, NX), jnp.float32) ** block_levels(streams_of[7], (LEV, NY, NX), ((1, 4), (2, 32)), -0.2, 0.2)), 0.05, 2.0)
    levels = place_ends(jax.random.randint(streams_of[8], (NY, NX), 0, LEV + 1), jax.random.fold_in(streams_of[8], 1), 0, LEV).astype(jnp.int32)
    return {"atmos_flux": atmos_flux, "remap_blocks": remap_blocks, "row_owner": row_owner, "row_target": row_target, "tracers": tracers, "east_vel": east_vel, "north_vel": north_vel, "mix_kappa": mix_kappa, "levels": levels}


sw_decay = 0.5
heat_coef = 0.5
fresh_coef = 0.5
stir_coef = 0.25
depth_decay = 0.5


def upwind(velocity, left_val, right_val, wet_left, wet_right):
    return (jnp.maximum(velocity, 0.0) * left_val + jnp.minimum(velocity, 0.0) * right_val) * (wet_left * wet_right)


def tridiagonal_solver(forcing_rhs, air_sea_link):
    depth_count = forcing_rhs.shape[0]
    zero_plane = jnp.zeros_like(forcing_rhs[0])
    gain_list = []
    offset_list = []
    for level_idx in range(depth_count):
        low_coef = air_sea_link[level_idx - 1] if level_idx > 0 else zero_plane
        up_coef = air_sea_link[level_idx] if level_idx < depth_count - 1 else zero_plane
        diagonal = 1.0 + low_coef + up_coef
        if level_idx > 0:
            denominator = diagonal - low_coef * gain_list[-1]
            numerator = forcing_rhs[level_idx] + low_coef * offset_list[-1]
        else:
            denominator = diagonal
            numerator = forcing_rhs[0]
        gain_list.append(up_coef / denominator)
        offset_list.append(numerator / denominator)
    solved = [offset_list[-1]]
    for level_idx in range(depth_count - 2, -1, -1):
        solved.append(offset_list[level_idx] + gain_list[level_idx] * solved[-1])
    return jnp.stack(solved[::-1], 0)


def step_tracers(ext_tracer, ext_east, ext_north, ext_wet, forcing, mix_kappa):
    eastward = upwind(ext_east[:, 1:-1, :-1], ext_tracer[:, :, 1:-1, :-1], ext_tracer[:, :, 1:-1, 1:],
                      ext_wet[:, 1:-1, :-1], ext_wet[:, 1:-1, 1:])
    poleward_speed = upwind(ext_north[:, :-1, 1:-1], ext_tracer[:, :, :-1, 1:-1], ext_tracer[:, :, 1:, 1:-1],
                       ext_wet[:, :-1, 1:-1], ext_wet[:, 1:, 1:-1])
    centre_cells = ext_tracer[:, :, 1:-1, 1:-1]
    wetness = ext_wet[:, 1:-1, 1:-1]
    carried_tracer = centre_cells - (eastward[..., 1:] - eastward[..., :-1]) - (poleward_speed[:, :, 1:, :] - poleward_speed[:, :, :-1, :])
    depth_count = wetness.shape[0]
    depth_rank = jnp.arange(depth_count, dtype=jnp.float32)
    sw_fraction = jnp.exp(-sw_decay * depth_rank) - jnp.exp(-sw_decay * (depth_rank + 1.0))
    heat_input = wetness * sw_fraction[:, None, None] * forcing[0][None]
    heat_top = heat_input[0] + wetness[0] * heat_coef * (forcing[1] + forcing[2] + forcing[3])
    heat_input = jnp.concatenate([heat_top[None], heat_input[1:]], 0)
    water_warmth = carried_tracer[0] + heat_input
    salt_surface = carried_tracer[1, 0] + wetness[0] * fresh_coef * forcing[4]
    salt_content = jnp.concatenate([salt_surface[None], carried_tracer[1, 1:]], 0)
    stirring = stir_coef * forcing[5] * forcing[5]
    air_sea_link = (mix_kappa[1:] + stirring[None] * jnp.exp(-depth_decay * depth_rank[1:])[:, None, None]) * wetness[1:]
    return jnp.stack([tridiagonal_solver(water_warmth, air_sea_link), tridiagonal_solver(salt_content, air_sea_link)], 0)


def extend(field):
    wrapped = jnp.concatenate([field[..., -1:], field, field[..., :1]], -1)
    zero_rows = jnp.zeros_like(wrapped[..., :1, :])
    return jnp.concatenate([zero_rows, wrapped, zero_rows], -2)


def reference(atmos_flux, remap_blocks, row_owner, row_target, tracers, east_vel, north_vel, mix_kappa, levels):
    owner_dev = row_owner[:, 0].astype(jnp.int32)
    lon_index = owner_dev // N_LAT
    lat_index = owner_dev % N_LAT
    global_row = (lat_index * CY + row_target).astype(jnp.int32)
    blocks_wide = remap_blocks.astype(jnp.float32)
    contrib = jnp.einsum("rfp,rpc->rfc", atmos_flux.astype(jnp.float32), blocks_wide, precision=lax.Precision.HIGHEST)
    forcing = jnp.zeros((NFLUX, NY, N_LON, CX), jnp.float32)
    forcing = forcing.at[:, global_row, lon_index, :].add(jnp.transpose(contrib, (1, 0, 2)))
    forcing = forcing.reshape(NFLUX, NY, NX)
    wetness = (jnp.arange(LEV, dtype=jnp.int32)[:, None, None] < levels[None]).astype(jnp.float32)
    tracers_next = step_tracers(extend(tracers), extend(east_vel), extend(north_vel), extend(wetness), forcing, mix_kappa)
    surface = tracers_next[:, 0].reshape(2, NY, N_LON, CX)
    row_state = surface[:, global_row, lon_index, :]
    atmos_state = jnp.einsum("fro,rpo->rfp", row_state, blocks_wide, precision=lax.Precision.HIGHEST)
    return tracers_next, atmos_state
```

```python
import math

import jax
import jax.numpy as jnp
from jax import lax
from jax.experimental import pallas as pl
from jax.experimental.pallas import tpu as pltpu
from jax.sharding import PartitionSpec as P

F32 = jnp.float32
BF16 = jnp.bfloat16

ROWS = 256
DEV = 128
CAP = 4
CELLS = 128
SENT = 4
BLOCK = CAP * SENT + 1
LEV = 8
CY = 32
CHUNKS = 8
PER = ROWS // CHUNKS

VMEM = pltpu.VMEM
SMEM = pltpu.SMEM


def split(x):
    high = x.astype(BF16)
    return high, (x - high.astype(F32)).astype(BF16)


def iota(shape, axis):
    return lax.broadcasted_iota(jnp.int32, shape, axis)


def params(mib):
    return pltpu.CompilerParams(vmem_limit_bytes=mib * 1024 * 1024)


def vmem_specs(count):
    return [pl.BlockSpec(memory_space=VMEM)] * count


def contrib_kernel(owner, target, flux_hbm, remap_hbm, send, slot_out, weights, flux, fields, slot_v, slot_s, sems, sem2):
    chunk_copies = [
        pltpu.make_async_copy(
            remap_hbm.at[pl.ds(c * PER, PER)], weights.at[pl.ds(c * PER, PER)], sems.at[c]
        )
        for c in range(CHUNKS)
    ]
    flux_copy = pltpu.make_async_copy(flux_hbm, flux, sem2.at[0])
    flux_copy.start()
    for copy in chunk_copies:
        copy.start()

    dev_iota = iota((DEV, 128), 0)
    own = owner[...]
    tgt = target[...].astype(F32) + 1.0
    member = jnp.concatenate(
        [(own[h : h + 1, :] == dev_iota).astype(F32) for h in range(2)], axis=1
    )
    before = (iota((ROWS, ROWS), 0) < iota((ROWS, ROWS), 1)).astype(BF16)
    earlier = jnp.dot(member.astype(BF16), before, preferred_element_type=F32)
    rank = jnp.sum(member * earlier, axis=0, keepdims=True)
    rank_i = rank.astype(jnp.int32)
    for h in range(2):
        slot_v[h : h + 1, :] = own[h : h + 1, :] * BLOCK + rank_i[:, h * 128 : (h + 1) * 128] * SENT
        slot_out[h : h + 1, :] = own[h : h + 1, :] * (2 * CAP) + rank_i[:, h * 128 : (h + 1) * 128] * 2
    slot_copy = pltpu.make_async_copy(slot_v, slot_s, sem2.at[1])
    slot_copy.start()
    tgt_row = jnp.concatenate([tgt[0:1, :], tgt[1:2, :]], axis=1)
    slot_tags = jnp.where(iota((DEV, ROWS), 0) == rank_i, tgt_row, 0.0).astype(BF16)
    tags = lax.dot_general(
        member.astype(BF16), slot_tags, (((1,), (1,)), ((), ())), preferred_element_type=F32
    )
    send[...] = jnp.zeros_like(send)
    send[pl.ds(CAP * SENT, DEV, stride=BLOCK), :] = tags

    flux_copy.wait()
    fields[pl.ds(0, ROWS, stride=SENT), :] = flux[0]
    fields[pl.ds(1, ROWS, stride=SENT), :] = flux[1] + flux[2] + flux[3]
    fields[pl.ds(2, ROWS, stride=SENT), :] = flux[4]
    fields[pl.ds(3, ROWS, stride=SENT), :] = flux[5]
    slot_copy.wait()

    def pair(r):
        high, low = split(fields[pl.ds(pl.multiple_of(r * SENT, 8), 8), :])
        left = jnp.concatenate([high, low], axis=0)
        right = jnp.concatenate([weights[r], weights[r + 1]], axis=1)
        both = jnp.dot(left, right, preferred_element_type=F32)
        both = both[:8] + both[8:]
        first = slot_s[r // 128, r % 128]
        second = slot_s[(r + 1) // 128, (r + 1) % 128]
        send[pl.ds(first, SENT), :] = both[:4, :CELLS]
        send[pl.ds(second, SENT), :] = both[4:, CELLS:]

    def chunk(c, carry):
        pltpu.make_async_copy(
            remap_hbm.at[pl.ds(c * PER, PER)], weights.at[pl.ds(c * PER, PER)], sems.at[c]
        ).wait()
        for i in range(0, PER, 2):
            pair(c * PER + i)
        return carry

    lax.fori_loop(0, CHUNKS, chunk, 0)


def contributions(row_owner, row_target, flux, remap):
    return pl.pallas_call(
        contrib_kernel,
        out_shape=(
            jax.ShapeDtypeStruct((DEV * BLOCK, CELLS), F32),
            jax.ShapeDtypeStruct((2, 128), jnp.int32),
        ),
        in_specs=vmem_specs(2) + [pl.BlockSpec(memory_space=pl.ANY)] * 2,
        out_specs=tuple(vmem_specs(2)),
        scratch_shapes=[
            VMEM((ROWS, 128, 128), BF16),
            VMEM((6, ROWS, 128), F32),
            VMEM((ROWS * SENT, 128), F32),
            VMEM((2, 128), jnp.int32),
            SMEM((2, 128), jnp.int32),
            pltpu.SemaphoreType.DMA((CHUNKS,)),
            pltpu.SemaphoreType.DMA((2,)),
        ],
        compiler_params=params(24),
        cost_estimate=pl.CostEstimate(flops=10**9, bytes_accessed=10_000_000, transcendentals=0),
        name="contrib",
    )(row_owner, row_target, flux, remap)


def edge_kernel(tracers, east_vel, north_vel, levels, to_east, to_west, to_north, to_south):
    lev = levels[...].astype(F32)
    lane = iota((CY, 128), 1)
    zero = jnp.zeros((CY, 128), F32)
    east, west = zero, zero
    planes = [tracers[p] for p in range(16)] + [lev] + [east_vel[k] for k in range(LEV)]
    for p, plane in enumerate(planes):
        east = jnp.where(lane == p, pltpu.roll(plane, (p + 1) % 128, 1), east)
        if p < 17:
            west = jnp.where(lane == p, plane if p == 0 else pltpu.roll(plane, p, 1), west)
    to_east[...] = east
    to_west[...] = west
    to_north[...] = zero
    to_south[...] = zero
    for p in range(16):
        to_north[p : p + 1, :] = tracers[p, CY - 1 : CY, :]
        to_south[p : p + 1, :] = tracers[p, 0:1, :]
    to_north[16:17, :] = lev[CY - 1 : CY]
    to_south[16:17, :] = lev[0:1]
    for k in range(LEV):
        to_north[17 + k : 18 + k, :] = north_vel[k, CY - 1 : CY, :]


def edges(tracers, east_vel, north_vel, levels):
    return pl.pallas_call(
        edge_kernel,
        out_shape=tuple(jax.ShapeDtypeStruct((CY, 128), F32) for _ in range(4)),
        in_specs=vmem_specs(4),
        out_specs=tuple(vmem_specs(4)),
        compiler_params=params(8),
        cost_estimate=pl.CostEstimate(flops=10**5, bytes_accessed=1_000_000, transcendentals=0),
        name="edges",
    )(tracers, east_vel, north_vel, levels)


def advect_kernel(tracers, east_vel, north_vel, levels, west_in, east_in, south_in, north_in, out):
    lane0 = iota((CY, 128), 1) == 0
    lane_last = iota((CY, 128), 1) == 127
    row0 = iota((CY, 128), 0) == 0
    row_last = iota((CY, 128), 0) == CY - 1
    lev = levels[...].astype(F32)

    def from_west(p):
        return west_in[...] if p == 0 else pltpu.roll(west_in[...], 128 - p, 1)

    def from_east(p):
        return pltpu.roll(east_in[...], 127 - p, 1)

    lev_w = from_west(16)
    lev_e = jnp.where(lane_last, from_east(16), pltpu.roll(lev, 127, 1))
    lev_s = south_in[16:17, :]
    lev_n = jnp.where(row_last, north_in[16:17, :], pltpu.roll(lev, CY - 1, 0))
    for k in range(LEV):
        depth = float(k)
        wet = (lev > depth).astype(F32)
        wet_w = wet * (lev_w > depth).astype(F32)
        wet_e = wet * (lev_e > depth).astype(F32)
        wet_s = wet * (lev_s > depth).astype(F32)
        wet_n = wet * (lev_n > depth).astype(F32)
        vel_e, vel_n = east_vel[k], north_vel[k]
        vel_w, vel_s = from_west(17 + k), south_in[17 + k : 18 + k, :]
        e_pos, e_neg = jnp.maximum(vel_e, 0.0), jnp.minimum(vel_e, 0.0)
        n_pos, n_neg = jnp.maximum(vel_n, 0.0), jnp.minimum(vel_n, 0.0)
        w_pos, w_neg = jnp.maximum(vel_w, 0.0), jnp.minimum(vel_w, 0.0)
        s_pos, s_neg = jnp.maximum(vel_s, 0.0), jnp.minimum(vel_s, 0.0)
        for t in range(2):
            p = t * LEV + k
            here = tracers[p]
            at_e = jnp.where(lane_last, from_east(p), pltpu.roll(here, 127, 1))
            at_n = jnp.where(row_last, north_in[p : p + 1, :], pltpu.roll(here, CY - 1, 0))
            flux_e = (e_pos * here + e_neg * at_e) * wet_e
            flux_n = (n_pos * here + n_neg * at_n) * wet_n
            edge_w = (w_pos * from_west(p) + w_neg * here) * wet_w
            edge_s = (s_pos * south_in[p : p + 1, :] + s_neg * here) * wet_s
            flux_w = jnp.where(lane0, edge_w, pltpu.roll(flux_e, 1, 1))
            flux_s = jnp.where(row0, edge_s, pltpu.roll(flux_n, 1, 0))
            out[p] = here - (flux_e - flux_w) - (flux_n - flux_s)


def advected(*args):
    return pl.pallas_call(
        advect_kernel,
        out_shape=jax.ShapeDtypeStruct((16, CY, 128), F32),
        in_specs=vmem_specs(8),
        out_specs=pl.BlockSpec(memory_space=VMEM),
        compiler_params=params(8),
        cost_estimate=pl.CostEstimate(flops=10**6, bytes_accessed=2_000_000, transcendentals=0),
        name="advect",
    )(*args)


def ocean_kernel(got, carried, kappa, levels, after, answer):
    tags = jnp.transpose(got[pl.ds(CAP * SENT, DEV, stride=BLOCK), :])
    labels = iota((CY, DEV), 0).astype(F32) + 1.0
    select = jnp.concatenate(
        [(tags[s : s + 1, :] == labels).astype(F32) for s in range(CAP)], axis=1
    ).astype(BF16)
    forcing = []
    for f in range(SENT):
        rows = jnp.concatenate(
            [got[pl.ds(s * SENT + f, DEV, stride=BLOCK), :] for s in range(CAP)], axis=0
        )
        high, low = split(rows)
        both = jnp.dot(select, jnp.concatenate([high, low], axis=1), preferred_element_type=F32)
        forcing.append(both[:, :CELLS] + both[:, CELLS:])
    short, surface_heat, fresh, wind = forcing
    lev = levels[...]
    stirring = 0.25 * wind * wind
    wet = [(lev > k).astype(F32) for k in range(LEV)]
    link = [None] + [
        (kappa[k] + stirring * math.exp(-0.5 * k)) * wet[k] for k in range(1, LEV)
    ]
    gains, offsets = [], []
    for k in range(LEV):
        fraction = math.exp(-0.5 * k) - math.exp(-0.5 * (k + 1))
        heat = wet[k] * (fraction * short)
        warmth, salt = carried[k] + heat, carried[LEV + k]
        if k == 0:
            warmth = warmth + 0.5 * wet[0] * surface_heat
            salt = salt + 0.5 * wet[0] * fresh
        diagonal = 1.0 if k == 0 else 1.0 + link[k]
        if k < LEV - 1:
            diagonal = diagonal + link[k + 1]
        if k > 0:
            diagonal = diagonal - link[k] * gains[-1]
            warmth = warmth + link[k] * offsets[-1][0]
            salt = salt + link[k] * offsets[-1][1]
        inverse = 1.0 / diagonal
        if k < LEV - 1:
            gains.append(link[k + 1] * inverse)
        offsets.append((warmth * inverse, salt * inverse))
    warmth, salt = offsets[-1]
    after[LEV - 1], after[2 * LEV - 1] = warmth, salt
    for k in range(LEV - 2, -1, -1):
        warmth = offsets[k][0] + gains[k] * warmth
        salt = offsets[k][1] + gains[k] * salt
        after[k], after[LEV + k] = warmth, salt
    high, low = split(jnp.concatenate([warmth, salt], axis=1))
    picked = lax.dot_general(
        select,
        jnp.concatenate([high, low], axis=1),
        (((0,), (0,)), ((), ())),
        preferred_element_type=F32,
    )
    for s in range(CAP):
        for f in range(2):
            rows = picked[s * DEV : (s + 1) * DEV]
            answer[:, 2 * s + f, :] = (
                rows[:, f * CELLS : (f + 1) * CELLS] + rows[:, (2 + f) * CELLS : (3 + f) * CELLS]
            )


def ocean(got, carried, kappa, levels):
    return pl.pallas_call(
        ocean_kernel,
        out_shape=(
            jax.ShapeDtypeStruct((16, CY, 128), F32),
            jax.ShapeDtypeStruct((DEV, 2 * CAP, CELLS), F32),
        ),
        in_specs=vmem_specs(4),
        out_specs=tuple(vmem_specs(2)),
        compiler_params=params(24),
        cost_estimate=pl.CostEstimate(flops=10**8, bytes_accessed=4_000_000, transcendentals=0),
        name="ocean",
    )(got, carried, kappa, levels)


def state_kernel(slots, returned, remap_hbm, out, weights, rows, sems):
    for c in range(CHUNKS):
        pltpu.make_async_copy(
            remap_hbm.at[pl.ds(c * PER, PER)], weights.at[pl.ds(c * PER, PER)], sems.at[c]
        ).start()

    def gather(g, carry):
        for i in range(16):
            r = g * 16 + i
            rows[pl.ds(2 * r, 2), :] = returned[pl.ds(slots[r // 128, r % 128], 2), :]
        return carry

    lax.fori_loop(0, ROWS // 16, gather, 0)

    def chunk(c, carry):
        pltpu.make_async_copy(
            remap_hbm.at[pl.ds(c * PER, PER)], weights.at[pl.ds(c * PER, PER)], sems.at[c]
        ).wait()
        for i in range(0, PER, 4):
            r = c * PER + i
            high, low = split(rows[pl.ds(pl.multiple_of(2 * r, 8), 8), :])
            left = jnp.concatenate([high, low], axis=0)
            right = weights[pl.ds(r, 4)].reshape(4 * 128, 128)
            four = lax.dot_general(
                left, right, (((1,), (1,)), ((), ())), preferred_element_type=F32
            )
            four = four[:8] + four[8:]
            for j in range(4):
                out[r + j] = four[2 * j : 2 * j + 2, j * 128 : (j + 1) * 128]
        return carry

    lax.fori_loop(0, CHUNKS, chunk, 0)


def state(slots, returned, remap):
    return pl.pallas_call(
        state_kernel,
        out_shape=jax.ShapeDtypeStruct((ROWS, 2, 128), F32),
        in_specs=[
            pl.BlockSpec(memory_space=SMEM),
            pl.BlockSpec(memory_space=VMEM),
            pl.BlockSpec(memory_space=pl.ANY),
        ],
        out_specs=pl.BlockSpec(memory_space=VMEM),
        scratch_shapes=[
            VMEM((ROWS, 128, 128), BF16),
            VMEM((2 * ROWS, 128), F32),
            pltpu.SemaphoreType.DMA((CHUNKS,)),
        ],
        compiler_params=params(24),
        cost_estimate=pl.CostEstimate(flops=10**9, bytes_accessed=9_000_000, transcendentals=0),
        name="state",
    )(slots, returned, remap)


def shifts(count, wraps):
    up = [(i, i + 1) for i in range(count - 1)] + ([(count - 1, 0)] if wraps else [])
    return up, [(b, a) for a, b in up]


def on_device(
    atmos_flux, remap_blocks, row_owner, row_target, tracers, east_vel, north_vel, mix_kappa, levels
):
    axes = ("lon", "lat")
    planes = tracers.reshape(2 * LEV, CY, CELLS)
    to_east, to_west, to_north, to_south = edges(planes, east_vel, north_vel, levels)
    eastward, westward = shifts(lax.axis_size("lon"), True)
    northward, southward = shifts(lax.axis_size("lat"), False)
    west_in = lax.ppermute(to_east, "lon", eastward)
    east_in = lax.ppermute(to_west, "lon", westward)
    south_in = lax.ppermute(to_north, "lat", northward)
    north_in = lax.ppermute(to_south, "lat", southward)
    send, slots = contributions(
        row_owner.reshape(2, 128),
        row_target.reshape(2, 128),
        jnp.transpose(atmos_flux, (1, 0, 2)),
        remap_blocks,
    )
    got = lax.all_to_all(
        send.reshape(DEV, BLOCK, 1, CELLS), axes, split_axis=0, concat_axis=0, tiled=True
    )
    carried = advected(planes, east_vel, north_vel, levels, west_in, east_in, south_in, north_in)
    after, answer = ocean(got.reshape(DEV * BLOCK, CELLS), carried, mix_kappa, levels)
    returned = lax.all_to_all(answer, axes, split_axis=0, concat_axis=0, tiled=True)
    atmos_state = state(slots, returned.reshape(DEV * 2 * CAP, CELLS), remap_blocks)
    return after.reshape(2, LEV, CY, CELLS), atmos_state


def solution(mesh):
    row = ("lon", "lat")
    in_specs = (
        P(row, None, None),
        P(row, None, None),
        P(row, None),
        P(row),
        P(None, None, "lat", "lon"),
        P(None, "lat", "lon"),
        P(None, "lat", "lon"),
        P(None, "lat", "lon"),
        P("lat", "lon"),
    )
    out_specs = (P(None, None, "lat", "lon"), P(row, None, None))
    return jax.shard_map(
        on_device, mesh=mesh, in_specs=in_specs, out_specs=out_specs, check_vma=False
    )
```

```python
import math

import jax
import jax.numpy as jnp
from jax import lax
from jax.experimental import pallas as pl
from jax.experimental.pallas import tpu as pltpu
from jax.sharding import PartitionSpec as P

F32 = jnp.float32
BF16 = jnp.bfloat16

ROWS = 256
DEV = 128
CAP = 4
CELLS = 128
SENT = 4
BLOCK = CAP * SENT + 1
LEV = 8
CY = 32
CHUNKS = 8
PER = ROWS // CHUNKS

VMEM = pltpu.VMEM
SMEM = pltpu.SMEM


def split(x):
    high = x.astype(BF16)
    return high, (x - high.astype(F32)).astype(BF16)


def iota(shape, axis):
    return lax.broadcasted_iota(jnp.int32, shape, axis)


def in_hbm(x):
    return pltpu.with_memory_space_constraint(x, pltpu.HBM)


def params(mib):
    return pltpu.CompilerParams(vmem_limit_bytes=mib * 1024 * 1024)


def vmem_specs(count):
    return [pl.BlockSpec(memory_space=VMEM)] * count


def contrib_kernel(
    owner, target, flux_hbm, remap_hbm, send, slot_out, weights, flux, fields, slot_v, slot_s, sems, sem2
):
    chunk_copies = [
        pltpu.make_async_copy(
            remap_hbm.at[pl.ds(c * PER, PER)], weights.at[pl.ds(c * PER, PER)], sems.at[c]
        )
        for c in range(CHUNKS)
    ]
    flux_copy = pltpu.make_async_copy(flux_hbm, flux, sem2.at[0])
    flux_copy.start()
    for copy in chunk_copies:
        copy.start()

    dev_iota = iota((DEV, 128), 0)
    own = owner[...]
    tgt = target[...].astype(F32) + 1.0
    member = jnp.concatenate(
        [(own[h : h + 1, :] == dev_iota).astype(F32) for h in range(2)], axis=1
    )
    before = (iota((ROWS, ROWS), 0) < iota((ROWS, ROWS), 1)).astype(BF16)
    earlier = jnp.dot(member.astype(BF16), before, preferred_element_type=F32)
    rank = jnp.sum(member * earlier, axis=0, keepdims=True)
    rank_i = rank.astype(jnp.int32)
    for h in range(2):
        slot_v[h : h + 1, :] = own[h : h + 1, :] * BLOCK + rank_i[:, h * 128 : (h + 1) * 128] * SENT
        slot_out[h : h + 1, :] = own[h : h + 1, :] * (2 * CAP) + rank_i[:, h * 128 : (h + 1) * 128] * 2
    slot_copy = pltpu.make_async_copy(slot_v, slot_s, sem2.at[1])
    slot_copy.start()
    tgt_row = jnp.concatenate([tgt[0:1, :], tgt[1:2, :]], axis=1)
    slot_tags = jnp.where(iota((DEV, ROWS), 0) == rank_i, tgt_row, 0.0).astype(BF16)
    tags = lax.dot_general(
        member.astype(BF16), slot_tags, (((1,), (1,)), ((), ())), preferred_element_type=F32
    )
    send[...] = jnp.zeros_like(send)
    send[pl.ds(CAP * SENT, DEV, stride=BLOCK), :] = tags

    flux_copy.wait()
    fields[pl.ds(0, ROWS, stride=SENT), :] = flux[0]
    fields[pl.ds(1, ROWS, stride=SENT), :] = flux[1] + flux[2] + flux[3]
    fields[pl.ds(2, ROWS, stride=SENT), :] = flux[4]
    fields[pl.ds(3, ROWS, stride=SENT), :] = flux[5]
    slot_copy.wait()

    def pair(r):
        high, low = split(fields[pl.ds(pl.multiple_of(r * SENT, 8), 8), :])
        left = jnp.concatenate([high, low], axis=0)
        right = jnp.concatenate([weights[r], weights[r + 1]], axis=1)
        both = jnp.dot(left, right, preferred_element_type=F32)
        both = both[:8] + both[8:]
        first = slot_s[r // 128, r % 128]
        second = slot_s[(r + 1) // 128, (r + 1) % 128]
        send[pl.ds(first, SENT), :] = both[:4, :CELLS]
        send[pl.ds(second, SENT), :] = both[4:, CELLS:]

    def chunk(c, carry):
        pltpu.make_async_copy(
            remap_hbm.at[pl.ds(c * PER, PER)], weights.at[pl.ds(c * PER, PER)], sems.at[c]
        ).wait()
        for i in range(0, PER, 2):
            pair(c * PER + i)
        return carry

    lax.fori_loop(0, CHUNKS, chunk, 0)


def contributions(row_owner, row_target, flux, remap):
    return pl.pallas_call(
        contrib_kernel,
        out_shape=(
            jax.ShapeDtypeStruct((DEV * BLOCK, CELLS), F32),
            jax.ShapeDtypeStruct((2, 128), jnp.int32),
        ),
        in_specs=vmem_specs(2) + [pl.BlockSpec(memory_space=pltpu.HBM)] * 2,
        out_specs=tuple(vmem_specs(2)),
        scratch_shapes=[
            VMEM((ROWS, 128, 128), BF16),
            VMEM((6, ROWS, 128), F32),
            VMEM((ROWS * SENT, 128), F32),
            VMEM((2, 128), jnp.int32),
            SMEM((2, 128), jnp.int32),
            pltpu.SemaphoreType.DMA((CHUNKS,)),
            pltpu.SemaphoreType.DMA((2,)),
        ],
        compiler_params=params(24),
        cost_estimate=pl.CostEstimate(flops=10**9, bytes_accessed=10_000_000, transcendentals=0),
        name="contrib",
    )(row_owner, row_target, flux, remap)


def edge_kernel(tracers, east_vel, north_vel, levels, to_east, to_west, to_north, to_south):
    lev = levels[...].astype(F32)
    lane = iota((CY, 128), 1)
    zero = jnp.zeros((CY, 128), F32)
    east, west = zero, zero
    planes = [tracers[p] for p in range(16)] + [lev] + [east_vel[k] for k in range(LEV)]
    for p, plane in enumerate(planes):
        east = jnp.where(lane == p, pltpu.roll(plane, (p + 1) % 128, 1), east)
        if p < 17:
            west = jnp.where(lane == p, plane if p == 0 else pltpu.roll(plane, p, 1), west)
    to_east[...] = east
    to_west[...] = west
    to_north[...] = zero
    to_south[...] = zero
    for p in range(16):
        to_north[p : p + 1, :] = tracers[p, CY - 1 : CY, :]
        to_south[p : p + 1, :] = tracers[p, 0:1, :]
    to_north[16:17, :] = lev[CY - 1 : CY]
    to_south[16:17, :] = lev[0:1]
    for k in range(LEV):
        to_north[17 + k : 18 + k, :] = north_vel[k, CY - 1 : CY, :]


def edges(tracers, east_vel, north_vel, levels):
    return pl.pallas_call(
        edge_kernel,
        out_shape=tuple(jax.ShapeDtypeStruct((CY, 128), F32) for _ in range(4)),
        in_specs=vmem_specs(4),
        out_specs=tuple(vmem_specs(4)),
        compiler_params=params(8),
        cost_estimate=pl.CostEstimate(flops=10**5, bytes_accessed=1_000_000, transcendentals=0),
        name="edges",
    )(tracers, east_vel, north_vel, levels)


def advect_kernel(tracers, east_vel, north_vel, levels, west_in, east_in, south_in, north_in, out):
    lane0 = iota((CY, 128), 1) == 0
    lane_last = iota((CY, 128), 1) == 127
    row0 = iota((CY, 128), 0) == 0
    row_last = iota((CY, 128), 0) == CY - 1
    lev = levels[...].astype(F32)

    def from_west(p):
        return west_in[...] if p == 0 else pltpu.roll(west_in[...], 128 - p, 1)

    def from_east(p):
        return pltpu.roll(east_in[...], 127 - p, 1)

    lev_w = from_west(16)
    lev_e = jnp.where(lane_last, from_east(16), pltpu.roll(lev, 127, 1))
    lev_s = south_in[16:17, :]
    lev_n = jnp.where(row_last, north_in[16:17, :], pltpu.roll(lev, CY - 1, 0))
    for k in range(LEV):
        depth = float(k)
        wet = (lev > depth).astype(F32)
        wet_w = wet * (lev_w > depth).astype(F32)
        wet_e = wet * (lev_e > depth).astype(F32)
        wet_s = wet * (lev_s > depth).astype(F32)
        wet_n = wet * (lev_n > depth).astype(F32)
        vel_e, vel_n = east_vel[k], north_vel[k]
        vel_w, vel_s = from_west(17 + k), south_in[17 + k : 18 + k, :]
        e_pos, e_neg = jnp.maximum(vel_e, 0.0), jnp.minimum(vel_e, 0.0)
        n_pos, n_neg = jnp.maximum(vel_n, 0.0), jnp.minimum(vel_n, 0.0)
        w_pos, w_neg = jnp.maximum(vel_w, 0.0), jnp.minimum(vel_w, 0.0)
        s_pos, s_neg = jnp.maximum(vel_s, 0.0), jnp.minimum(vel_s, 0.0)
        for t in range(2):
            p = t * LEV + k
            here = tracers[p]
            at_e = jnp.where(lane_last, from_east(p), pltpu.roll(here, 127, 1))
            at_n = jnp.where(row_last, north_in[p : p + 1, :], pltpu.roll(here, CY - 1, 0))
            flux_e = (e_pos * here + e_neg * at_e) * wet_e
            flux_n = (n_pos * here + n_neg * at_n) * wet_n
            edge_w = (w_pos * from_west(p) + w_neg * here) * wet_w
            edge_s = (s_pos * south_in[p : p + 1, :] + s_neg * here) * wet_s
            flux_w = jnp.where(lane0, edge_w, pltpu.roll(flux_e, 1, 1))
            flux_s = jnp.where(row0, edge_s, pltpu.roll(flux_n, 1, 0))
            out[p] = here - (flux_e - flux_w) - (flux_n - flux_s)


def advected(*args):
    return pl.pallas_call(
        advect_kernel,
        out_shape=jax.ShapeDtypeStruct((16, CY, 128), F32),
        in_specs=vmem_specs(8),
        out_specs=pl.BlockSpec(memory_space=VMEM),
        compiler_params=params(8),
        cost_estimate=pl.CostEstimate(flops=10**6, bytes_accessed=2_000_000, transcendentals=0),
        name="advect",
    )(*args)


def ocean_kernel(got, carried, kappa, levels, after, answer):
    tags = jnp.transpose(got[pl.ds(CAP * SENT, DEV, stride=BLOCK), :])
    labels = iota((CY, DEV), 0).astype(F32) + 1.0
    select = jnp.concatenate(
        [(tags[s : s + 1, :] == labels).astype(F32) for s in range(CAP)], axis=1
    ).astype(BF16)
    forcing = []
    for f in range(SENT):
        rows = jnp.concatenate(
            [got[pl.ds(s * SENT + f, DEV, stride=BLOCK), :] for s in range(CAP)], axis=0
        )
        high, low = split(rows)
        both = jnp.dot(select, jnp.concatenate([high, low], axis=1), preferred_element_type=F32)
        forcing.append(both[:, :CELLS] + both[:, CELLS:])
    short, surface_heat, fresh, wind = forcing
    lev = levels[...]
    stirring = 0.25 * wind * wind
    wet = [(lev > k).astype(F32) for k in range(LEV)]
    link = [None] + [
        (kappa[k] + stirring * math.exp(-0.5 * k)) * wet[k] for k in range(1, LEV)
    ]
    gains, offsets = [], []
    for k in range(LEV):
        fraction = math.exp(-0.5 * k) - math.exp(-0.5 * (k + 1))
        heat = wet[k] * (fraction * short)
        warmth, salt = carried[k] + heat, carried[LEV + k]
        if k == 0:
            warmth = warmth + 0.5 * wet[0] * surface_heat
            salt = salt + 0.5 * wet[0] * fresh
        diagonal = 1.0 if k == 0 else 1.0 + link[k]
        if k < LEV - 1:
            diagonal = diagonal + link[k + 1]
        if k > 0:
            diagonal = diagonal - link[k] * gains[-1]
            warmth = warmth + link[k] * offsets[-1][0]
            salt = salt + link[k] * offsets[-1][1]
        inverse = 1.0 / diagonal
        if k < LEV - 1:
            gains.append(link[k + 1] * inverse)
        offsets.append((warmth * inverse, salt * inverse))
    warmth, salt = offsets[-1]
    after[LEV - 1], after[2 * LEV - 1] = warmth, salt
    for k in range(LEV - 2, -1, -1):
        warmth = offsets[k][0] + gains[k] * warmth
        salt = offsets[k][1] + gains[k] * salt
        after[k], after[LEV + k] = warmth, salt
    high, low = split(jnp.concatenate([warmth, salt], axis=1))
    picked = lax.dot_general(
        select,
        jnp.concatenate([high, low], axis=1),
        (((0,), (0,)), ((), ())),
        preferred_element_type=F32,
    )
    for s in range(CAP):
        for f in range(2):
            rows = picked[s * DEV : (s + 1) * DEV]
            answer[:, 2 * s + f, :] = (
                rows[:, f * CELLS : (f + 1) * CELLS] + rows[:, (2 + f) * CELLS : (3 + f) * CELLS]
            )


def ocean(got, carried, kappa, levels):
    return pl.pallas_call(
        ocean_kernel,
        out_shape=(
            jax.ShapeDtypeStruct((16, CY, 128), F32),
            jax.ShapeDtypeStruct((DEV, 2 * CAP, CELLS), F32),
        ),
        in_specs=vmem_specs(4),
        out_specs=tuple(vmem_specs(2)),
        compiler_params=params(24),
        cost_estimate=pl.CostEstimate(flops=10**8, bytes_accessed=4_000_000, transcendentals=0),
        name="ocean",
    )(got, carried, kappa, levels)


def state_kernel(slots, returned, remap_hbm, out, weights, rows, sems):
    for c in range(CHUNKS):
        pltpu.make_async_copy(
            remap_hbm.at[pl.ds(c * PER, PER)], weights.at[pl.ds(c * PER, PER)], sems.at[c]
        ).start()

    def gather(g, carry):
        for i in range(16):
            r = g * 16 + i
            rows[pl.ds(2 * r, 2), :] = returned[pl.ds(slots[r // 128, r % 128], 2), :]
        return carry

    lax.fori_loop(0, ROWS // 16, gather, 0)

    def chunk(c, carry):
        pltpu.make_async_copy(
            remap_hbm.at[pl.ds(c * PER, PER)], weights.at[pl.ds(c * PER, PER)], sems.at[c]
        ).wait()
        for i in range(0, PER, 4):
            r = c * PER + i
            high, low = split(rows[pl.ds(pl.multiple_of(2 * r, 8), 8), :])
            left = jnp.concatenate([high, low], axis=0)
            right = weights[pl.ds(r, 4)].reshape(4 * 128, 128)
            four = lax.dot_general(
                left, right, (((1,), (1,)), ((), ())), preferred_element_type=F32
            )
            four = four[:8] + four[8:]
            for j in range(4):
                out[r + j] = four[2 * j : 2 * j + 2, j * 128 : (j + 1) * 128]
        return carry

    lax.fori_loop(0, CHUNKS, chunk, 0)


def state(slots, returned, remap):
    return pl.pallas_call(
        state_kernel,
        out_shape=jax.ShapeDtypeStruct((ROWS, 2, 128), F32),
        in_specs=[
            pl.BlockSpec(memory_space=SMEM),
            pl.BlockSpec(memory_space=VMEM),
            pl.BlockSpec(memory_space=pltpu.HBM),
        ],
        out_specs=pl.BlockSpec(memory_space=VMEM),
        scratch_shapes=[
            VMEM((ROWS, 128, 128), BF16),
            VMEM((2 * ROWS, 128), F32),
            pltpu.SemaphoreType.DMA((CHUNKS,)),
        ],
        compiler_params=params(24),
        cost_estimate=pl.CostEstimate(flops=10**9, bytes_accessed=9_000_000, transcendentals=0),
        name="state",
    )(slots, returned, remap)


def shifts(count, wraps):
    up = [(i, i + 1) for i in range(count - 1)] + ([(count - 1, 0)] if wraps else [])
    return up, [(b, a) for a, b in up]


def on_device(
    atmos_flux, remap_blocks, row_owner, row_target, tracers, east_vel, north_vel, mix_kappa, levels
):
    axes = ("lon", "lat")
    planes = tracers.reshape(2 * LEV, CY, CELLS)
    to_east, to_west, to_north, to_south = edges(planes, east_vel, north_vel, levels)
    eastward, westward = shifts(lax.axis_size("lon"), True)
    northward, southward = shifts(lax.axis_size("lat"), False)
    west_in = lax.ppermute(to_east, "lon", eastward)
    east_in = lax.ppermute(to_west, "lon", westward)
    south_in = lax.ppermute(to_north, "lat", northward)
    north_in = lax.ppermute(to_south, "lat", southward)
    send, slots = contributions(
        row_owner.reshape(2, 128),
        row_target.reshape(2, 128),
        in_hbm(jnp.transpose(atmos_flux, (1, 0, 2))),
        in_hbm(remap_blocks),
    )
    got = lax.all_to_all(
        send.reshape(DEV, BLOCK, 1, CELLS), axes, split_axis=0, concat_axis=0, tiled=True
    )
    carried = advected(planes, east_vel, north_vel, levels, west_in, east_in, south_in, north_in)
    after, answer = ocean(got.reshape(DEV * BLOCK, CELLS), carried, mix_kappa, levels)
    returned = lax.all_to_all(answer, axes, split_axis=0, concat_axis=0, tiled=True)
    atmos_state = state(slots, returned.reshape(DEV * 2 * CAP, CELLS), in_hbm(remap_blocks))
    return after.reshape(2, LEV, CY, CELLS), atmos_state


def solution(mesh):
    row = ("lon", "lat")
    in_specs = (
        P(row, None, None),
        P(row, None, None),
        P(row, None),
        P(row),
        P(None, None, "lat", "lon"),
        P(None, "lat", "lon"),
        P(None, "lat", "lon"),
        P(None, "lat", "lon"),
        P("lat", "lon"),
    )
    out_specs = (P(None, None, "lat", "lon"), P(row, None, None))
    return jax.shard_map(
        on_device, mesh=mesh, in_specs=in_specs, out_specs=out_specs, check_vma=False
    )
```

```python
import math

import jax
import jax.numpy as jnp
from jax import lax
from jax.experimental import pallas as pl
from jax.experimental.pallas import tpu as pltpu
from jax.sharding import PartitionSpec as P

F32 = jnp.float32
BF16 = jnp.bfloat16

ROWS = 256
DEV = 128
CAP = 4
CELLS = 128
SENT = 4
BLOCK = CAP * SENT + 1
LEV = 8
CY = 32
CONTRIB_SIZES = (16, 32, 48, 64, 96)
STATE_SIZES = (64, 64, 64, 64)

VMEM = pltpu.VMEM
SMEM = pltpu.SMEM


def split(x):
    high = x.astype(BF16)
    return high, (x - high.astype(F32)).astype(BF16)


def iota(shape, axis):
    return lax.broadcasted_iota(jnp.int32, shape, axis)


def spans(sizes):
    return [(sum(sizes[:i]), size) for i, size in enumerate(sizes)]


def block_copies(remap_hbm, weights, sems, sizes):
    return [
        pltpu.make_async_copy(
            remap_hbm.at[pl.ds(start, size)], weights.at[pl.ds(start, size)], sems.at[i]
        )
        for i, (start, size) in enumerate(spans(sizes))
    ]


def in_hbm(x):
    return pltpu.with_memory_space_constraint(x, pltpu.HBM)


def params(mib):
    return pltpu.CompilerParams(vmem_limit_bytes=mib * 1024 * 1024)


def vmem_specs(count):
    return [pl.BlockSpec(memory_space=VMEM)] * count


def contrib_kernel(
    owner_hbm,
    target_hbm,
    flux_hbm,
    remap_hbm,
    send,
    slot_out,
    weights,
    flux,
    fields,
    owner,
    target,
    slot_v,
    slot_s,
    sems,
    sem2,
):
    chunk_copies = block_copies(remap_hbm, weights, sems, CONTRIB_SIZES)
    owner_copy = pltpu.make_async_copy(owner_hbm, owner, sem2.at[2])
    target_copy = pltpu.make_async_copy(target_hbm, target, sem2.at[3])
    flux_copy = pltpu.make_async_copy(flux_hbm, flux, sem2.at[0])
    owner_copy.start()
    target_copy.start()
    flux_copy.start()
    for copy in chunk_copies:
        copy.start()
    send[...] = jnp.zeros_like(send)
    owner_copy.wait()
    target_copy.wait()

    dev_iota = iota((DEV, 128), 0)
    own = owner[...]
    tgt = target[...].astype(F32) + 1.0
    member = jnp.concatenate(
        [(own[h : h + 1, :] == dev_iota).astype(F32) for h in range(2)], axis=1
    )
    before = (iota((ROWS, ROWS), 0) < iota((ROWS, ROWS), 1)).astype(BF16)
    earlier = jnp.dot(member.astype(BF16), before, preferred_element_type=F32)
    rank = jnp.sum(member * earlier, axis=0, keepdims=True)
    rank_i = rank.astype(jnp.int32)
    for h in range(2):
        slot_v[h : h + 1, :] = own[h : h + 1, :] * BLOCK + rank_i[:, h * 128 : (h + 1) * 128] * SENT
        slot_out[h : h + 1, :] = own[h : h + 1, :] * (2 * CAP) + rank_i[:, h * 128 : (h + 1) * 128] * 2
    slot_copy = pltpu.make_async_copy(slot_v, slot_s, sem2.at[1])
    slot_copy.start()
    tgt_row = jnp.concatenate([tgt[0:1, :], tgt[1:2, :]], axis=1)
    slot_tags = jnp.where(iota((DEV, ROWS), 0) == rank_i, tgt_row, 0.0).astype(BF16)
    tags = lax.dot_general(
        member.astype(BF16), slot_tags, (((1,), (1,)), ((), ())), preferred_element_type=F32
    )
    send[pl.ds(CAP * SENT, DEV, stride=BLOCK), :] = tags

    flux_copy.wait()
    fields[pl.ds(0, ROWS, stride=SENT), :] = flux[0]
    fields[pl.ds(1, ROWS, stride=SENT), :] = flux[1] + flux[2] + flux[3]
    fields[pl.ds(2, ROWS, stride=SENT), :] = flux[4]
    fields[pl.ds(3, ROWS, stride=SENT), :] = flux[5]
    slot_copy.wait()

    def pair(r):
        high, low = split(fields[pl.ds(pl.multiple_of(r * SENT, 8), 8), :])
        left = jnp.concatenate([high, low], axis=0)
        right = jnp.concatenate([weights[r], weights[r + 1]], axis=1)
        both = jnp.dot(left, right, preferred_element_type=F32)
        both = both[:8] + both[8:]
        first = slot_s[r // 128, r % 128]
        second = slot_s[(r + 1) // 128, (r + 1) % 128]
        send[pl.ds(first, SENT), :] = both[:4, :CELLS]
        send[pl.ds(second, SENT), :] = both[4:, CELLS:]

    for copy, (start, size) in zip(chunk_copies, spans(CONTRIB_SIZES)):
        copy.wait()
        for r in range(start, start + size, 2):
            pair(r)


def contributions(row_owner, row_target, flux, remap):
    return pl.pallas_call(
        contrib_kernel,
        out_shape=(
            jax.ShapeDtypeStruct((DEV * BLOCK, CELLS), F32),
            jax.ShapeDtypeStruct((2, 128), jnp.int32),
        ),
        in_specs=[pl.BlockSpec(memory_space=pltpu.HBM)] * 4,
        out_specs=tuple(vmem_specs(2)),
        scratch_shapes=[
            VMEM((ROWS, 128, 128), BF16),
            VMEM((6, ROWS, 128), F32),
            VMEM((ROWS * SENT, 128), F32),
            VMEM((2, 128), jnp.int32),
            VMEM((2, 128), jnp.int32),
            VMEM((2, 128), jnp.int32),
            SMEM((2, 128), jnp.int32),
            pltpu.SemaphoreType.DMA((len(CONTRIB_SIZES),)),
            pltpu.SemaphoreType.DMA((4,)),
        ],
        compiler_params=params(24),
        cost_estimate=pl.CostEstimate(flops=10**9, bytes_accessed=10_000_000, transcendentals=0),
        name="contrib",
    )(row_owner, row_target, flux, remap)


def edge_kernel(tracers, east_vel, north_vel, levels, to_east, to_west, to_north, to_south):
    lev = levels[...].astype(F32)
    lane = iota((CY, 128), 1)
    zero = jnp.zeros((CY, 128), F32)
    east, west = zero, zero
    planes = [tracers[p] for p in range(16)] + [lev] + [east_vel[k] for k in range(LEV)]
    for p, plane in enumerate(planes):
        east = jnp.where(lane == p, pltpu.roll(plane, (p + 1) % 128, 1), east)
        if p < 17:
            west = jnp.where(lane == p, plane if p == 0 else pltpu.roll(plane, p, 1), west)
    to_east[...] = east
    to_west[...] = west
    to_north[...] = zero
    to_south[...] = zero
    for p in range(16):
        to_north[p : p + 1, :] = tracers[p, CY - 1 : CY, :]
        to_south[p : p + 1, :] = tracers[p, 0:1, :]
    to_north[16:17, :] = lev[CY - 1 : CY]
    to_south[16:17, :] = lev[0:1]
    for k in range(LEV):
        to_north[17 + k : 18 + k, :] = north_vel[k, CY - 1 : CY, :]


def edges(tracers, east_vel, north_vel, levels):
    return pl.pallas_call(
        edge_kernel,
        out_shape=tuple(jax.ShapeDtypeStruct((CY, 128), F32) for _ in range(4)),
        in_specs=vmem_specs(4),
        out_specs=tuple(vmem_specs(4)),
        compiler_params=params(8),
        cost_estimate=pl.CostEstimate(flops=10**5, bytes_accessed=1_000_000, transcendentals=0),
        name="edges",
    )(tracers, east_vel, north_vel, levels)


def advect_kernel(tracers, east_vel, north_vel, levels, west_in, east_in, south_in, north_in, out):
    lane0 = iota((CY, 128), 1) == 0
    lane_last = iota((CY, 128), 1) == 127
    row0 = iota((CY, 128), 0) == 0
    row_last = iota((CY, 128), 0) == CY - 1
    lev = levels[...].astype(F32)

    def from_west(p):
        return west_in[...] if p == 0 else pltpu.roll(west_in[...], 128 - p, 1)

    def from_east(p):
        return pltpu.roll(east_in[...], 127 - p, 1)

    lev_w = from_west(16)
    lev_e = jnp.where(lane_last, from_east(16), pltpu.roll(lev, 127, 1))
    lev_s = south_in[16:17, :]
    lev_n = jnp.where(row_last, north_in[16:17, :], pltpu.roll(lev, CY - 1, 0))
    for k in range(LEV):
        depth = float(k)
        wet = (lev > depth).astype(F32)
        wet_w = wet * (lev_w > depth).astype(F32)
        wet_e = wet * (lev_e > depth).astype(F32)
        wet_s = wet * (lev_s > depth).astype(F32)
        wet_n = wet * (lev_n > depth).astype(F32)
        vel_e, vel_n = east_vel[k], north_vel[k]
        vel_w, vel_s = from_west(17 + k), south_in[17 + k : 18 + k, :]
        e_pos, e_neg = jnp.maximum(vel_e, 0.0), jnp.minimum(vel_e, 0.0)
        n_pos, n_neg = jnp.maximum(vel_n, 0.0), jnp.minimum(vel_n, 0.0)
        w_pos, w_neg = jnp.maximum(vel_w, 0.0), jnp.minimum(vel_w, 0.0)
        s_pos, s_neg = jnp.maximum(vel_s, 0.0), jnp.minimum(vel_s, 0.0)
        for t in range(2):
            p = t * LEV + k
            here = tracers[p]
            at_e = jnp.where(lane_last, from_east(p), pltpu.roll(here, 127, 1))
            at_n = jnp.where(row_last, north_in[p : p + 1, :], pltpu.roll(here, CY - 1, 0))
            flux_e = (e_pos * here + e_neg * at_e) * wet_e
            flux_n = (n_pos * here + n_neg * at_n) * wet_n
            edge_w = (w_pos * from_west(p) + w_neg * here) * wet_w
            edge_s = (s_pos * south_in[p : p + 1, :] + s_neg * here) * wet_s
            flux_w = jnp.where(lane0, edge_w, pltpu.roll(flux_e, 1, 1))
            flux_s = jnp.where(row0, edge_s, pltpu.roll(flux_n, 1, 0))
            out[p] = here - (flux_e - flux_w) - (flux_n - flux_s)


def advected(*args):
    return pl.pallas_call(
        advect_kernel,
        out_shape=jax.ShapeDtypeStruct((16, CY, 128), F32),
        in_specs=vmem_specs(8),
        out_specs=pl.BlockSpec(memory_space=VMEM),
        compiler_params=params(8),
        cost_estimate=pl.CostEstimate(flops=10**6, bytes_accessed=2_000_000, transcendentals=0),
        name="advect",
    )(*args)


def ocean_kernel(got, carried, kappa, levels, after, answer):
    tags = jnp.transpose(got[pl.ds(CAP * SENT, DEV, stride=BLOCK), :])
    labels = iota((CY, DEV), 0).astype(F32) + 1.0
    select = jnp.concatenate(
        [(tags[s : s + 1, :] == labels).astype(F32) for s in range(CAP)], axis=1
    ).astype(BF16)
    forcing = []
    for f in range(SENT):
        rows = jnp.concatenate(
            [got[pl.ds(s * SENT + f, DEV, stride=BLOCK), :] for s in range(CAP)], axis=0
        )
        high, low = split(rows)
        both = jnp.dot(select, jnp.concatenate([high, low], axis=1), preferred_element_type=F32)
        forcing.append(both[:, :CELLS] + both[:, CELLS:])
    short, surface_heat, fresh, wind = forcing
    lev = levels[...]
    stirring = 0.25 * wind * wind
    wet = [(lev > k).astype(F32) for k in range(LEV)]
    link = [None] + [
        (kappa[k] + stirring * math.exp(-0.5 * k)) * wet[k] for k in range(1, LEV)
    ]
    gains, offsets = [], []
    for k in range(LEV):
        fraction = math.exp(-0.5 * k) - math.exp(-0.5 * (k + 1))
        heat = wet[k] * (fraction * short)
        warmth, salt = carried[k] + heat, carried[LEV + k]
        if k == 0:
            warmth = warmth + 0.5 * wet[0] * surface_heat
            salt = salt + 0.5 * wet[0] * fresh
        diagonal = 1.0 if k == 0 else 1.0 + link[k]
        if k < LEV - 1:
            diagonal = diagonal + link[k + 1]
        if k > 0:
            diagonal = diagonal - link[k] * gains[-1]
            warmth = warmth + link[k] * offsets[-1][0]
            salt = salt + link[k] * offsets[-1][1]
        inverse = 1.0 / diagonal
        if k < LEV - 1:
            gains.append(link[k + 1] * inverse)
        offsets.append((warmth * inverse, salt * inverse))
    warmth, salt = offsets[-1]
    after[LEV - 1], after[2 * LEV - 1] = warmth, salt
    for k in range(LEV - 2, -1, -1):
        warmth = offsets[k][0] + gains[k] * warmth
        salt = offsets[k][1] + gains[k] * salt
        after[k], after[LEV + k] = warmth, salt
    high, low = split(jnp.concatenate([warmth, salt], axis=1))
    picked = lax.dot_general(
        select,
        jnp.concatenate([high, low], axis=1),
        (((0,), (0,)), ((), ())),
        preferred_element_type=F32,
    )
    for s in range(CAP):
        for f in range(2):
            rows = picked[s * DEV : (s + 1) * DEV]
            answer[:, 2 * s + f, :] = (
                rows[:, f * CELLS : (f + 1) * CELLS] + rows[:, (2 + f) * CELLS : (3 + f) * CELLS]
            )


def ocean(got, carried, kappa, levels):
    return pl.pallas_call(
        ocean_kernel,
        out_shape=(
            jax.ShapeDtypeStruct((16, CY, 128), F32),
            jax.ShapeDtypeStruct((DEV, 2 * CAP, CELLS), F32),
        ),
        in_specs=vmem_specs(4),
        out_specs=tuple(vmem_specs(2)),
        compiler_params=params(24),
        cost_estimate=pl.CostEstimate(flops=10**8, bytes_accessed=4_000_000, transcendentals=0),
        name="ocean",
    )(got, carried, kappa, levels)


def state_kernel(slots, returned, remap_hbm, out, weights, rows, sems):
    chunk_copies = block_copies(remap_hbm, weights, sems, STATE_SIZES)
    for copy in chunk_copies:
        copy.start()

    for r in range(ROWS):
        rows[2 * r : 2 * r + 2, :] = returned[pl.ds(slots[r // 128, r % 128], 2), :]
    for copy, (start, size) in zip(chunk_copies, spans(STATE_SIZES)):
        copy.wait()
        for r in range(start, start + size, 4):
            high, low = split(rows[2 * r : 2 * r + 8, :])
            left = jnp.concatenate([high, low], axis=0)
            right = weights[r : r + 4].reshape(4 * 128, 128)
            four = lax.dot_general(
                left, right, (((1,), (1,)), ((), ())), preferred_element_type=F32
            )
            four = four[:8] + four[8:]
            for j in range(4):
                out[r + j] = four[2 * j : 2 * j + 2, j * 128 : (j + 1) * 128]


def state(slots, returned, remap):
    return pl.pallas_call(
        state_kernel,
        out_shape=jax.ShapeDtypeStruct((ROWS, 2, 128), F32),
        in_specs=[
            pl.BlockSpec(memory_space=SMEM),
            pl.BlockSpec(memory_space=VMEM),
            pl.BlockSpec(memory_space=pltpu.HBM),
        ],
        out_specs=pl.BlockSpec(memory_space=VMEM),
        scratch_shapes=[
            VMEM((ROWS, 128, 128), BF16),
            VMEM((2 * ROWS, 128), F32),
            pltpu.SemaphoreType.DMA((len(STATE_SIZES),)),
        ],
        compiler_params=params(24),
        cost_estimate=pl.CostEstimate(flops=10**9, bytes_accessed=9_000_000, transcendentals=0),
        name="state",
    )(slots, returned, remap)


def shifts(count, wraps):
    up = [(i, i + 1) for i in range(count - 1)] + ([(count - 1, 0)] if wraps else [])
    return up, [(b, a) for a, b in up]


def on_device(
    atmos_flux, remap_blocks, row_owner, row_target, tracers, east_vel, north_vel, mix_kappa, levels
):
    axes = ("lon", "lat")
    planes = tracers.reshape(2 * LEV, CY, CELLS)
    to_east, to_west, to_north, to_south = edges(planes, east_vel, north_vel, levels)
    eastward, westward = shifts(lax.axis_size("lon"), True)
    northward, southward = shifts(lax.axis_size("lat"), False)
    west_in = lax.ppermute(to_east, "lon", eastward)
    east_in = lax.ppermute(to_west, "lon", westward)
    south_in = lax.ppermute(to_north, "lat", northward)
    north_in = lax.ppermute(to_south, "lat", southward)
    send, slots = contributions(
        in_hbm(row_owner.reshape(2, 128)),
        in_hbm(row_target.reshape(2, 128)),
        in_hbm(jnp.transpose(atmos_flux, (1, 0, 2))),
        in_hbm(remap_blocks),
    )
    got = lax.all_to_all(
        send.reshape(DEV, BLOCK, 1, CELLS), axes, split_axis=0, concat_axis=0, tiled=True
    )
    carried = advected(planes, east_vel, north_vel, levels, west_in, east_in, south_in, north_in)
    after, answer = ocean(got.reshape(DEV * BLOCK, CELLS), carried, mix_kappa, levels)
    returned = lax.all_to_all(answer, axes, split_axis=0, concat_axis=0, tiled=True)
    atmos_state = state(slots, returned.reshape(DEV * 2 * CAP, CELLS), in_hbm(remap_blocks))
    return after.reshape(2, LEV, CY, CELLS), atmos_state


def solution(mesh):
    row = ("lon", "lat")
    in_specs = (
        P(row, None, None),
        P(row, None, None),
        P(row, None),
        P(row),
        P(None, None, "lat", "lon"),
        P(None, "lat", "lon"),
        P(None, "lat", "lon"),
        P(None, "lat", "lon"),
        P("lat", "lon"),
    )
    out_specs = (P(None, None, "lat", "lon"), P(row, None, None))
    return jax.shard_map(
        on_device, mesh=mesh, in_specs=in_specs, out_specs=out_specs, check_vma=False
    )
```

```python
import math

import jax
import jax.numpy as jnp
from jax import lax
from jax.experimental import pallas as pl
from jax.experimental.pallas import tpu as pltpu
from jax.sharding import PartitionSpec as P

F32 = jnp.float32
BF16 = jnp.bfloat16

ROWS = 256
DEV = 128
CAP = 4
CELLS = 128
SENT = 4
BLOCK = CAP * SENT + 1
LEV = 8
CY = 32
CONTRIB_SIZES = (32, 48, 80, 96)
NEAR = 32
FAR_SIZES = (48, 80, 96)

VMEM = pltpu.VMEM
SMEM = pltpu.SMEM


def split(x):
    high = x.astype(BF16)
    return high, (x - high.astype(F32)).astype(BF16)


def iota(shape, axis):
    return lax.broadcasted_iota(jnp.int32, shape, axis)


def spans(sizes):
    return [(sum(sizes[:i]), size) for i, size in enumerate(sizes)]


def block_copies(remap_hbm, near, far, sems, sizes, skipped=0):
    copies = []
    for i, (start, size) in enumerate(spans(sizes)):
        first = skipped + start
        inside = first < NEAR
        target = near.at[pl.ds(first, size)] if inside else far.at[pl.ds(first - NEAR, size)]
        copies.append(pltpu.make_async_copy(remap_hbm.at[pl.ds(first, size)], target, sems.at[i]))
    return copies


def in_hbm(x):
    return pltpu.with_memory_space_constraint(x, pltpu.HBM)


def params(mib):
    return pltpu.CompilerParams(vmem_limit_bytes=mib * 1024 * 1024)


def vmem_specs(count):
    return [pl.BlockSpec(memory_space=VMEM)] * count


def contrib_kernel(
    owner_hbm,
    target_hbm,
    flux_hbm,
    remap_hbm,
    send,
    slot_out,
    near,
    far,
    flux,
    fields,
    owner,
    target,
    slot_v,
    slot_s,
    sems,
    sem2,
):
    chunk_copies = block_copies(remap_hbm, near, far, sems, CONTRIB_SIZES)
    owner_copy = pltpu.make_async_copy(owner_hbm, owner, sem2.at[2])
    target_copy = pltpu.make_async_copy(target_hbm, target, sem2.at[3])
    flux_copy = pltpu.make_async_copy(flux_hbm, flux, sem2.at[0])
    owner_copy.start()
    target_copy.start()
    flux_copy.start()
    for copy in chunk_copies:
        copy.start()
    send[...] = jnp.zeros_like(send)
    owner_copy.wait()
    target_copy.wait()

    dev_iota = iota((DEV, 128), 0)
    own = owner[...]
    tgt = target[...].astype(F32) + 1.0
    member = jnp.concatenate(
        [(own[h : h + 1, :] == dev_iota).astype(F32) for h in range(2)], axis=1
    )
    before = (iota((ROWS, ROWS), 0) < iota((ROWS, ROWS), 1)).astype(BF16)
    earlier = jnp.dot(member.astype(BF16), before, preferred_element_type=F32)
    rank = jnp.sum(member * earlier, axis=0, keepdims=True)
    rank_i = rank.astype(jnp.int32)
    for h in range(2):
        slot_v[h : h + 1, :] = own[h : h + 1, :] * BLOCK + rank_i[:, h * 128 : (h + 1) * 128] * SENT
        slot_out[h : h + 1, :] = own[h : h + 1, :] * (2 * CAP) + rank_i[:, h * 128 : (h + 1) * 128] * 2
    slot_copy = pltpu.make_async_copy(slot_v, slot_s, sem2.at[1])
    slot_copy.start()
    tgt_row = jnp.concatenate([tgt[0:1, :], tgt[1:2, :]], axis=1)
    slot_tags = jnp.where(iota((DEV, ROWS), 0) == rank_i, tgt_row, 0.0).astype(BF16)
    tags = lax.dot_general(
        member.astype(BF16), slot_tags, (((1,), (1,)), ((), ())), preferred_element_type=F32
    )
    send[pl.ds(CAP * SENT, DEV, stride=BLOCK), :] = tags

    flux_copy.wait()
    fields[pl.ds(0, ROWS, stride=SENT), :] = flux[0]
    fields[pl.ds(1, ROWS, stride=SENT), :] = flux[1] + flux[2] + flux[3]
    fields[pl.ds(2, ROWS, stride=SENT), :] = flux[4]
    fields[pl.ds(3, ROWS, stride=SENT), :] = flux[5]
    slot_copy.wait()

    def pair(r):
        high, low = split(fields[pl.ds(pl.multiple_of(r * SENT, 8), 8), :])
        left = jnp.concatenate([high, low], axis=0)
        blocks = [near[i] if i < NEAR else far[i - NEAR] for i in (r, r + 1)]
        right = jnp.concatenate(blocks, axis=1)
        both = jnp.dot(left, right, preferred_element_type=F32)
        both = both[:8] + both[8:]
        first = slot_s[r // 128, r % 128]
        second = slot_s[(r + 1) // 128, (r + 1) % 128]
        send[pl.ds(first, SENT), :] = both[:4, :CELLS]
        send[pl.ds(second, SENT), :] = both[4:, CELLS:]

    for copy, (start, size) in zip(chunk_copies, spans(CONTRIB_SIZES)):
        copy.wait()
        for r in range(start, start + size, 2):
            pair(r)


def contributions(row_owner, row_target, flux, remap):
    return pl.pallas_call(
        contrib_kernel,
        out_shape=(
            jax.ShapeDtypeStruct((DEV * BLOCK, CELLS), F32),
            jax.ShapeDtypeStruct((2, 128), jnp.int32),
            VMEM((NEAR, 128, 128), BF16),
        ),
        in_specs=[pl.BlockSpec(memory_space=pltpu.HBM)] * 4,
        out_specs=tuple(vmem_specs(3)),
        scratch_shapes=[
            VMEM((ROWS - NEAR, 128, 128), BF16),
            VMEM((6, ROWS, 128), F32),
            VMEM((ROWS * SENT, 128), F32),
            VMEM((2, 128), jnp.int32),
            VMEM((2, 128), jnp.int32),
            VMEM((2, 128), jnp.int32),
            SMEM((2, 128), jnp.int32),
            pltpu.SemaphoreType.DMA((len(CONTRIB_SIZES),)),
            pltpu.SemaphoreType.DMA((4,)),
        ],
        compiler_params=params(24),
        cost_estimate=pl.CostEstimate(flops=10**9, bytes_accessed=10_000_000, transcendentals=0),
        name="contrib",
    )(row_owner, row_target, flux, remap)


def edge_kernel(tracers, east_vel, north_vel, levels, to_east, to_west, to_north, to_south):
    lev = levels[...].astype(F32)
    lane = iota((CY, 128), 1)
    zero = jnp.zeros((CY, 128), F32)
    east, west = zero, zero
    planes = [tracers[p] for p in range(16)] + [lev] + [east_vel[k] for k in range(LEV)]
    for p, plane in enumerate(planes):
        east = jnp.where(lane == p, pltpu.roll(plane, (p + 1) % 128, 1), east)
        if p < 17:
            west = jnp.where(lane == p, plane if p == 0 else pltpu.roll(plane, p, 1), west)
    to_east[...] = east
    to_west[...] = west
    to_north[...] = zero
    to_south[...] = zero
    for p in range(16):
        to_north[p : p + 1, :] = tracers[p, CY - 1 : CY, :]
        to_south[p : p + 1, :] = tracers[p, 0:1, :]
    to_north[16:17, :] = lev[CY - 1 : CY]
    to_south[16:17, :] = lev[0:1]
    for k in range(LEV):
        to_north[17 + k : 18 + k, :] = north_vel[k, CY - 1 : CY, :]


def edges(tracers, east_vel, north_vel, levels):
    return pl.pallas_call(
        edge_kernel,
        out_shape=tuple(jax.ShapeDtypeStruct((CY, 128), F32) for _ in range(4)),
        in_specs=vmem_specs(4),
        out_specs=tuple(vmem_specs(4)),
        compiler_params=params(8),
        cost_estimate=pl.CostEstimate(flops=10**5, bytes_accessed=1_000_000, transcendentals=0),
        name="edges",
    )(tracers, east_vel, north_vel, levels)


def advect_kernel(tracers, east_vel, north_vel, levels, west_in, east_in, south_in, north_in, out):
    lane0 = iota((CY, 128), 1) == 0
    lane_last = iota((CY, 128), 1) == 127
    row0 = iota((CY, 128), 0) == 0
    row_last = iota((CY, 128), 0) == CY - 1
    lev = levels[...].astype(F32)

    def from_west(p):
        return west_in[...] if p == 0 else pltpu.roll(west_in[...], 128 - p, 1)

    def from_east(p):
        return pltpu.roll(east_in[...], 127 - p, 1)

    lev_w = from_west(16)
    lev_e = jnp.where(lane_last, from_east(16), pltpu.roll(lev, 127, 1))
    lev_s = south_in[16:17, :]
    lev_n = jnp.where(row_last, north_in[16:17, :], pltpu.roll(lev, CY - 1, 0))
    for k in range(LEV):
        depth = float(k)
        wet = (lev > depth).astype(F32)
        wet_w = wet * (lev_w > depth).astype(F32)
        wet_e = wet * (lev_e > depth).astype(F32)
        wet_s = wet * (lev_s > depth).astype(F32)
        wet_n = wet * (lev_n > depth).astype(F32)
        vel_e, vel_n = east_vel[k], north_vel[k]
        vel_w, vel_s = from_west(17 + k), south_in[17 + k : 18 + k, :]
        e_pos, e_neg = jnp.maximum(vel_e, 0.0), jnp.minimum(vel_e, 0.0)
        n_pos, n_neg = jnp.maximum(vel_n, 0.0), jnp.minimum(vel_n, 0.0)
        w_pos, w_neg = jnp.maximum(vel_w, 0.0), jnp.minimum(vel_w, 0.0)
        s_pos, s_neg = jnp.maximum(vel_s, 0.0), jnp.minimum(vel_s, 0.0)
        for t in range(2):
            p = t * LEV + k
            here = tracers[p]
            at_e = jnp.where(lane_last, from_east(p), pltpu.roll(here, 127, 1))
            at_n = jnp.where(row_last, north_in[p : p + 1, :], pltpu.roll(here, CY - 1, 0))
            flux_e = (e_pos * here + e_neg * at_e) * wet_e
            flux_n = (n_pos * here + n_neg * at_n) * wet_n
            edge_w = (w_pos * from_west(p) + w_neg * here) * wet_w
            edge_s = (s_pos * south_in[p : p + 1, :] + s_neg * here) * wet_s
            flux_w = jnp.where(lane0, edge_w, pltpu.roll(flux_e, 1, 1))
            flux_s = jnp.where(row0, edge_s, pltpu.roll(flux_n, 1, 0))
            out[p] = here - (flux_e - flux_w) - (flux_n - flux_s)


def advected(*args):
    return pl.pallas_call(
        advect_kernel,
        out_shape=jax.ShapeDtypeStruct((16, CY, 128), F32),
        in_specs=vmem_specs(8),
        out_specs=pl.BlockSpec(memory_space=VMEM),
        compiler_params=params(8),
        cost_estimate=pl.CostEstimate(flops=10**6, bytes_accessed=2_000_000, transcendentals=0),
        name="advect",
    )(*args)


def ocean_kernel(got, carried, kappa, levels, after, answer):
    tags = jnp.transpose(got[pl.ds(CAP * SENT, DEV, stride=BLOCK), :])
    labels = iota((CY, DEV), 0).astype(F32) + 1.0
    select = jnp.concatenate(
        [(tags[s : s + 1, :] == labels).astype(F32) for s in range(CAP)], axis=1
    ).astype(BF16)
    forcing = []
    for f in range(SENT):
        rows = jnp.concatenate(
            [got[pl.ds(s * SENT + f, DEV, stride=BLOCK), :] for s in range(CAP)], axis=0
        )
        high, low = split(rows)
        both = jnp.dot(select, jnp.concatenate([high, low], axis=1), preferred_element_type=F32)
        forcing.append(both[:, :CELLS] + both[:, CELLS:])
    short, surface_heat, fresh, wind = forcing
    lev = levels[...]
    stirring = 0.25 * wind * wind
    wet = [(lev > k).astype(F32) for k in range(LEV)]
    link = [None] + [
        (kappa[k] + stirring * math.exp(-0.5 * k)) * wet[k] for k in range(1, LEV)
    ]
    gains, offsets = [], []
    for k in range(LEV):
        fraction = math.exp(-0.5 * k) - math.exp(-0.5 * (k + 1))
        heat = wet[k] * (fraction * short)
        warmth, salt = carried[k] + heat, carried[LEV + k]
        if k == 0:
            warmth = warmth + 0.5 * wet[0] * surface_heat
            salt = salt + 0.5 * wet[0] * fresh
        diagonal = 1.0 if k == 0 else 1.0 + link[k]
        if k < LEV - 1:
            diagonal = diagonal + link[k + 1]
        if k > 0:
            diagonal = diagonal - link[k] * gains[-1]
            warmth = warmth + link[k] * offsets[-1][0]
            salt = salt + link[k] * offsets[-1][1]
        inverse = 1.0 / diagonal
        if k < LEV - 1:
            gains.append(link[k + 1] * inverse)
        offsets.append((warmth * inverse, salt * inverse))
    warmth, salt = offsets[-1]
    after[LEV - 1], after[2 * LEV - 1] = warmth, salt
    for k in range(LEV - 2, -1, -1):
        warmth = offsets[k][0] + gains[k] * warmth
        salt = offsets[k][1] + gains[k] * salt
        after[k], after[LEV + k] = warmth, salt
    high, low = split(jnp.concatenate([warmth, salt], axis=1))
    picked = lax.dot_general(
        select,
        jnp.concatenate([high, low], axis=1),
        (((0,), (0,)), ((), ())),
        preferred_element_type=F32,
    )
    for s in range(CAP):
        for f in range(2):
            rows = picked[s * DEV : (s + 1) * DEV]
            answer[:, 2 * s + f, :] = (
                rows[:, f * CELLS : (f + 1) * CELLS] + rows[:, (2 + f) * CELLS : (3 + f) * CELLS]
            )


def ocean(got, carried, kappa, levels):
    return pl.pallas_call(
        ocean_kernel,
        out_shape=(
            jax.ShapeDtypeStruct((16, CY, 128), F32),
            jax.ShapeDtypeStruct((DEV, 2 * CAP, CELLS), F32),
        ),
        in_specs=vmem_specs(4),
        out_specs=tuple(vmem_specs(2)),
        compiler_params=params(24),
        cost_estimate=pl.CostEstimate(flops=10**8, bytes_accessed=4_000_000, transcendentals=0),
        name="ocean",
    )(got, carried, kappa, levels)


def state_kernel(slots_in, returned, near, remap_hbm, out_hbm, far, rows, out, slots, sems, out_sems, sem):
    far_copies = block_copies(remap_hbm, near, far, sems, FAR_SIZES, NEAR)
    slot_copy = pltpu.make_async_copy(slots_in, slots, sem)
    slot_copy.start()
    for copy in far_copies:
        copy.start()
    slot_copy.wait()
    for r in range(ROWS):
        rows[2 * r : 2 * r + 2, :] = returned[pl.ds(slots[r // 128, r % 128], 2), :]

    def four_rows(r, blocks):
        high, low = split(rows[2 * r : 2 * r + 8, :])
        left = jnp.concatenate([high, low], axis=0)
        four = lax.dot_general(
            left,
            blocks.reshape(4 * 128, 128),
            (((1,), (1,)), ((), ())),
            preferred_element_type=F32,
        )
        four = four[:8] + four[8:]
        for j in range(4):
            out[r + j] = four[2 * j : 2 * j + 2, j * 128 : (j + 1) * 128]

    out_copies = []

    def hand_on(start, size):
        part = pl.ds(start, size)
        copy = pltpu.make_async_copy(out.at[part], out_hbm.at[part], out_sems.at[len(out_copies)])
        copy.start()
        out_copies.append(copy)

    for r in range(0, NEAR, 4):
        four_rows(r, near[r : r + 4])
    hand_on(0, NEAR)
    for copy, (start, size) in zip(far_copies, spans(FAR_SIZES)):
        copy.wait()
        for r in range(start, start + size, 4):
            four_rows(NEAR + r, far[r : r + 4])
        hand_on(NEAR + start, size)
    for copy in out_copies:
        copy.wait()


def state(slots, returned, near, remap):
    return pl.pallas_call(
        state_kernel,
        out_shape=pltpu.HBM((ROWS, 2, 128), F32),
        in_specs=vmem_specs(3) + [pl.BlockSpec(memory_space=pltpu.HBM)],
        out_specs=pl.BlockSpec(memory_space=pltpu.HBM),
        scratch_shapes=[
            VMEM((ROWS - NEAR, 128, 128), BF16),
            VMEM((2 * ROWS, 128), F32),
            VMEM((ROWS, 2, 128), F32),
            SMEM((2, 128), jnp.int32),
            pltpu.SemaphoreType.DMA((len(FAR_SIZES),)),
            pltpu.SemaphoreType.DMA((len(FAR_SIZES) + 1,)),
            pltpu.SemaphoreType.DMA,
        ],
        compiler_params=params(20),
        cost_estimate=pl.CostEstimate(flops=10**9, bytes_accessed=9_000_000, transcendentals=0),
        name="state",
    )(slots, returned, near, remap)


def shifts(count, wraps):
    up = [(i, i + 1) for i in range(count - 1)] + ([(count - 1, 0)] if wraps else [])
    return up, [(b, a) for a, b in up]


def on_device(
    atmos_flux, remap_blocks, row_owner, row_target, tracers, east_vel, north_vel, mix_kappa, levels
):
    axes = ("lon", "lat")
    planes = tracers.reshape(2 * LEV, CY, CELLS)
    to_east, to_west, to_north, to_south = edges(planes, east_vel, north_vel, levels)
    eastward, westward = shifts(lax.axis_size("lon"), True)
    northward, southward = shifts(lax.axis_size("lat"), False)
    west_in = lax.ppermute(to_east, "lon", eastward)
    east_in = lax.ppermute(to_west, "lon", westward)
    south_in = lax.ppermute(to_north, "lat", northward)
    north_in = lax.ppermute(to_south, "lat", southward)
    send, slots, near = contributions(
        in_hbm(row_owner.reshape(2, 128)),
        in_hbm(row_target.reshape(2, 128)),
        in_hbm(jnp.transpose(atmos_flux, (1, 0, 2))),
        in_hbm(remap_blocks),
    )
    got = lax.all_to_all(
        send.reshape(DEV, BLOCK, 1, CELLS), axes, split_axis=0, concat_axis=0, tiled=True
    )
    carried = advected(planes, east_vel, north_vel, levels, west_in, east_in, south_in, north_in)
    after, answer = ocean(got.reshape(DEV * BLOCK, CELLS), carried, mix_kappa, levels)
    returned = lax.all_to_all(answer, axes, split_axis=0, concat_axis=0, tiled=True)
    atmos_state = state(
        slots,
        returned.reshape(DEV * 2 * CAP, CELLS),
        pltpu.with_memory_space_constraint(near, VMEM),
        in_hbm(remap_blocks),
    )
    return after.reshape(2, LEV, CY, CELLS), atmos_state


def solution(mesh):
    row = ("lon", "lat")
    in_specs = (
        P(row, None, None),
        P(row, None, None),
        P(row, None),
        P(row),
        P(None, None, "lat", "lon"),
        P(None, "lat", "lon"),
        P(None, "lat", "lon"),
        P(None, "lat", "lon"),
        P("lat", "lon"),
    )
    out_specs = (P(None, None, "lat", "lon"), P(row, None, None))
    return jax.shard_map(
        on_device, mesh=mesh, in_specs=in_specs, out_specs=out_specs, check_vma=False
    )
```

```python
import math

import jax
import jax.numpy as jnp
from jax import lax
from jax.experimental import pallas as pl
from jax.experimental.pallas import tpu as pltpu
from jax.sharding import PartitionSpec as P

F32 = jnp.float32
BF16 = jnp.bfloat16

ROWS = 256
DEV = 128
CAP = 4
CELLS = 128
SENT = 4
BLOCK = CAP * SENT + 1
LEV = 8
CY = 32
CONTRIB_SIZES = (32, 48, 80, 96)
NEAR = 32
FAR_SIZES = (48, 80, 96)

VMEM = pltpu.VMEM
SMEM = pltpu.SMEM


def split(x):
    high = x.astype(BF16)
    return high, (x - high.astype(F32)).astype(BF16)


def iota(shape, axis):
    return lax.broadcasted_iota(jnp.int32, shape, axis)


def spans(sizes):
    return [(sum(sizes[:i]), size) for i, size in enumerate(sizes)]


def block_copies(remap_hbm, near, far, sems, sizes, skipped=0):
    copies = []
    for i, (start, size) in enumerate(spans(sizes)):
        first = skipped + start
        inside = first < NEAR
        target = near.at[pl.ds(first, size)] if inside else far.at[pl.ds(first - NEAR, size)]
        copies.append(pltpu.make_async_copy(remap_hbm.at[pl.ds(first, size)], target, sems.at[i]))
    return copies


def in_hbm(x):
    return pltpu.with_memory_space_constraint(x, pltpu.HBM)


def params(mib):
    return pltpu.CompilerParams(vmem_limit_bytes=mib * 1024 * 1024)


def vmem_specs(count):
    return [pl.BlockSpec(memory_space=VMEM)] * count


def contrib_kernel(
    owner_hbm,
    target_hbm,
    flux_hbm,
    remap_hbm,
    send,
    slot_out,
    near,
    far,
    flux,
    fields,
    owner,
    target,
    slot_v,
    slot_s,
    sems,
    sem2,
):
    chunk_copies = block_copies(remap_hbm, near, far, sems, CONTRIB_SIZES)
    owner_copy = pltpu.make_async_copy(owner_hbm, owner, sem2.at[2])
    target_copy = pltpu.make_async_copy(target_hbm, target, sem2.at[3])
    flux_copy = pltpu.make_async_copy(flux_hbm, flux, sem2.at[0])
    owner_copy.start()
    target_copy.start()
    flux_copy.start()
    for copy in chunk_copies:
        copy.start()
    send[...] = jnp.zeros_like(send)
    owner_copy.wait()
    target_copy.wait()

    dev_iota = iota((DEV, 128), 0)
    own = owner[...]
    tgt = target[...].astype(F32) + 1.0
    member = jnp.concatenate(
        [(own[h : h + 1, :] == dev_iota).astype(F32) for h in range(2)], axis=1
    )
    before = (iota((ROWS, ROWS), 0) < iota((ROWS, ROWS), 1)).astype(BF16)
    earlier = jnp.dot(member.astype(BF16), before, preferred_element_type=F32)
    rank = jnp.sum(member * earlier, axis=0, keepdims=True)
    rank_i = rank.astype(jnp.int32)
    for h in range(2):
        slot_v[h : h + 1, :] = own[h : h + 1, :] * BLOCK + rank_i[:, h * 128 : (h + 1) * 128] * SENT
        slot_out[h : h + 1, :] = own[h : h + 1, :] * (2 * CAP) + rank_i[:, h * 128 : (h + 1) * 128] * 2
    slot_copy = pltpu.make_async_copy(slot_v, slot_s, sem2.at[1])
    slot_copy.start()
    tgt_row = jnp.concatenate([tgt[0:1, :], tgt[1:2, :]], axis=1)
    slot_tags = jnp.where(iota((DEV, ROWS), 0) == rank_i, tgt_row, 0.0).astype(BF16)
    tags = lax.dot_general(
        member.astype(BF16), slot_tags, (((1,), (1,)), ((), ())), preferred_element_type=F32
    )
    send[pl.ds(CAP * SENT, DEV, stride=BLOCK), :] = tags

    flux_copy.wait()
    fields[pl.ds(0, ROWS, stride=SENT), :] = flux[0]
    fields[pl.ds(1, ROWS, stride=SENT), :] = flux[1] + flux[2] + flux[3]
    fields[pl.ds(2, ROWS, stride=SENT), :] = flux[4]
    fields[pl.ds(3, ROWS, stride=SENT), :] = flux[5]
    slot_copy.wait()

    def pair(r):
        high, low = split(fields[pl.ds(pl.multiple_of(r * SENT, 8), 8), :])
        left = jnp.concatenate([high, low], axis=0)
        blocks = [near[i] if i < NEAR else far[i - NEAR] for i in (r, r + 1)]
        right = jnp.concatenate(blocks, axis=1)
        both = jnp.dot(left, right, preferred_element_type=F32)
        both = both[:8] + both[8:]
        first = slot_s[r // 128, r % 128]
        second = slot_s[(r + 1) // 128, (r + 1) % 128]
        send[pl.ds(first, SENT), :] = both[:4, :CELLS]
        send[pl.ds(second, SENT), :] = both[4:, CELLS:]

    for copy, (start, size) in zip(chunk_copies, spans(CONTRIB_SIZES)):
        copy.wait()
        for r in range(start, start + size, 2):
            pair(r)


def contributions(row_owner, row_target, flux, remap):
    return pl.pallas_call(
        contrib_kernel,
        out_shape=(
            jax.ShapeDtypeStruct((DEV * BLOCK, CELLS), F32),
            jax.ShapeDtypeStruct((2, 128), jnp.int32),
            VMEM((NEAR, 128, 128), BF16),
        ),
        in_specs=[pl.BlockSpec(memory_space=pltpu.HBM)] * 4,
        out_specs=tuple(vmem_specs(3)),
        scratch_shapes=[
            VMEM((ROWS - NEAR, 128, 128), BF16),
            VMEM((6, ROWS, 128), F32),
            VMEM((ROWS * SENT, 128), F32),
            VMEM((2, 128), jnp.int32),
            VMEM((2, 128), jnp.int32),
            VMEM((2, 128), jnp.int32),
            SMEM((2, 128), jnp.int32),
            pltpu.SemaphoreType.DMA((len(CONTRIB_SIZES),)),
            pltpu.SemaphoreType.DMA((4,)),
        ],
        compiler_params=params(24),
        cost_estimate=pl.CostEstimate(flops=10**9, bytes_accessed=10_000_000, transcendentals=0),
        name="contrib",
    )(row_owner, row_target, flux, remap)


def edge_kernel(tracers, east_vel, north_vel, levels, to_east, to_west, to_north, to_south):
    lev = levels[...].astype(F32)
    lane = iota((CY, 128), 1)
    zero = jnp.zeros((CY, 128), F32)
    east, west = zero, zero
    planes = [tracers[p] for p in range(16)] + [lev] + [east_vel[k] for k in range(LEV)]
    for p, plane in enumerate(planes):
        east = jnp.where(lane == p, pltpu.roll(plane, (p + 1) % 128, 1), east)
        if p < 17:
            west = jnp.where(lane == p, plane if p == 0 else pltpu.roll(plane, p, 1), west)
    to_east[...] = east
    to_west[...] = west
    to_north[...] = zero
    to_south[...] = zero
    for p in range(16):
        to_north[p : p + 1, :] = tracers[p, CY - 1 : CY, :]
        to_south[p : p + 1, :] = tracers[p, 0:1, :]
    to_north[16:17, :] = lev[CY - 1 : CY]
    to_south[16:17, :] = lev[0:1]
    for k in range(LEV):
        to_north[17 + k : 18 + k, :] = north_vel[k, CY - 1 : CY, :]


def edges(tracers, east_vel, north_vel, levels):
    return pl.pallas_call(
        edge_kernel,
        out_shape=tuple(jax.ShapeDtypeStruct((CY, 128), F32) for _ in range(4)),
        in_specs=vmem_specs(4),
        out_specs=tuple(vmem_specs(4)),
        compiler_params=params(8),
        cost_estimate=pl.CostEstimate(flops=10**5, bytes_accessed=1_000_000, transcendentals=0),
        name="edges",
    )(tracers, east_vel, north_vel, levels)


def advect_kernel(tracers, east_vel, north_vel, levels, out):
    lane_last = iota((CY, 128), 1) == 127
    row_last = iota((CY, 128), 0) == CY - 1
    lev = levels[...].astype(F32)
    lev_e = jnp.where(lane_last, 0.0, pltpu.roll(lev, 127, 1))
    lev_n = jnp.where(row_last, 0.0, pltpu.roll(lev, CY - 1, 0))
    for k in range(LEV):
        depth = float(k)
        wet = (lev > depth).astype(F32)
        wet_e = wet * (lev_e > depth).astype(F32)
        wet_n = wet * (lev_n > depth).astype(F32)
        vel_e, vel_n = east_vel[k], north_vel[k]
        e_pos, e_neg = jnp.maximum(vel_e, 0.0), jnp.minimum(vel_e, 0.0)
        n_pos, n_neg = jnp.maximum(vel_n, 0.0), jnp.minimum(vel_n, 0.0)
        for t in range(2):
            p = t * LEV + k
            here = tracers[p]
            flux_e = (e_pos * here + e_neg * pltpu.roll(here, 127, 1)) * wet_e
            flux_n = (n_pos * here + n_neg * pltpu.roll(here, CY - 1, 0)) * wet_n
            out[p] = here - (flux_e - pltpu.roll(flux_e, 1, 1)) - (flux_n - pltpu.roll(flux_n, 1, 0))


def advected(*args):
    return pl.pallas_call(
        advect_kernel,
        out_shape=jax.ShapeDtypeStruct((16, CY, 128), F32),
        in_specs=vmem_specs(4),
        out_specs=pl.BlockSpec(memory_space=VMEM),
        compiler_params=params(8),
        cost_estimate=pl.CostEstimate(flops=10**6, bytes_accessed=2_000_000, transcendentals=0),
        name="advect",
    )(*args)


def face(vel, low, high, lev_low, lev_high, depth):
    wet = (lev_low > depth).astype(F32) * (lev_high > depth).astype(F32)
    return (jnp.maximum(vel, 0.0) * low + jnp.minimum(vel, 0.0) * high) * wet


def side_face(low, high):
    lane = iota((CY, 128), 1)
    packed = low[...]
    vel = jnp.where(lane < LEV, pltpu.roll(packed, 128 - 17, 1), pltpu.roll(packed, 128 - 9, 1))
    return face(
        vel, packed, high[...], low[:, 16:17], high[:, 16:17], (lane % LEV).astype(F32)
    )


def end_face(low, high):
    vel = jnp.concatenate([low[17 : 17 + LEV, :]] * 2, axis=0)
    depth = (iota((2 * LEV, 128), 0) % LEV).astype(F32)
    return face(
        vel, low[0 : 2 * LEV, :], high[0 : 2 * LEV, :], low[16:17, :], high[16:17, :], depth
    )


def ocean_kernel(
    got,
    inner,
    kappa,
    levels,
    to_east,
    to_west,
    to_north,
    to_south,
    west_in,
    east_in,
    south_in,
    north_in,
    after,
    answer,
):
    lane, row = iota((CY, 128), 1), iota((CY, 128), 0)
    from_west, to_next = side_face(west_in, to_west), side_face(to_east, east_in)
    from_south, to_top = end_face(south_in, to_south), end_face(to_north, north_in)
    carried = []
    for p in range(2 * LEV):
        west = from_west if p == 0 else pltpu.roll(from_west, 128 - p, 1)
        sides = jnp.where(lane == 0, west, 0.0)
        sides = jnp.where(lane == 127, -pltpu.roll(to_next, 127 - p, 1), sides)
        ends = jnp.where(row == 0, from_south[p : p + 1, :], 0.0)
        ends = jnp.where(row == CY - 1, -to_top[p : p + 1, :], ends)
        carried.append(inner[p] + sides + ends)
    tags = jnp.transpose(got[pl.ds(CAP * SENT, DEV, stride=BLOCK), :])
    labels = iota((CY, DEV), 0).astype(F32) + 1.0
    select = jnp.concatenate(
        [(tags[s : s + 1, :] == labels).astype(F32) for s in range(CAP)], axis=1
    ).astype(BF16)
    forcing = []
    for f in range(SENT):
        rows = jnp.concatenate(
            [got[pl.ds(s * SENT + f, DEV, stride=BLOCK), :] for s in range(CAP)], axis=0
        )
        high, low = split(rows)
        both = jnp.dot(select, jnp.concatenate([high, low], axis=1), preferred_element_type=F32)
        forcing.append(both[:, :CELLS] + both[:, CELLS:])
    short, surface_heat, fresh, wind = forcing
    lev = levels[...]
    stirring = 0.25 * wind * wind
    wet = [(lev > k).astype(F32) for k in range(LEV)]
    link = [None] + [
        (kappa[k] + stirring * math.exp(-0.5 * k)) * wet[k] for k in range(1, LEV)
    ]
    gains, offsets = [], []
    for k in range(LEV):
        fraction = math.exp(-0.5 * k) - math.exp(-0.5 * (k + 1))
        heat = wet[k] * (fraction * short)
        warmth, salt = carried[k] + heat, carried[LEV + k]
        if k == 0:
            warmth = warmth + 0.5 * wet[0] * surface_heat
            salt = salt + 0.5 * wet[0] * fresh
        diagonal = 1.0 if k == 0 else 1.0 + link[k]
        if k < LEV - 1:
            diagonal = diagonal + link[k + 1]
        if k > 0:
            diagonal = diagonal - link[k] * gains[-1]
            warmth = warmth + link[k] * offsets[-1][0]
            salt = salt + link[k] * offsets[-1][1]
        inverse = 1.0 / diagonal
        if k < LEV - 1:
            gains.append(link[k + 1] * inverse)
        offsets.append((warmth * inverse, salt * inverse))
    warmth, salt = offsets[-1]
    after[LEV - 1], after[2 * LEV - 1] = warmth, salt
    for k in range(LEV - 2, -1, -1):
        warmth = offsets[k][0] + gains[k] * warmth
        salt = offsets[k][1] + gains[k] * salt
        after[k], after[LEV + k] = warmth, salt
    high, low = split(jnp.concatenate([warmth, salt], axis=1))
    picked = lax.dot_general(
        select,
        jnp.concatenate([high, low], axis=1),
        (((0,), (0,)), ((), ())),
        preferred_element_type=F32,
    )
    for s in range(CAP):
        for f in range(2):
            rows = picked[s * DEV : (s + 1) * DEV]
            answer[:, 2 * s + f, :] = (
                rows[:, f * CELLS : (f + 1) * CELLS] + rows[:, (2 + f) * CELLS : (3 + f) * CELLS]
            )


def ocean(*args):
    return pl.pallas_call(
        ocean_kernel,
        out_shape=(
            jax.ShapeDtypeStruct((16, CY, 128), F32),
            jax.ShapeDtypeStruct((DEV, 2 * CAP, CELLS), F32),
        ),
        in_specs=vmem_specs(12),
        out_specs=tuple(vmem_specs(2)),
        compiler_params=params(24),
        cost_estimate=pl.CostEstimate(flops=10**8, bytes_accessed=4_000_000, transcendentals=0),
        name="ocean",
    )(*args)


def state_kernel(slots_in, returned, near, remap_hbm, out_hbm, far, rows, out, slots, sems, out_sems, sem):
    far_copies = block_copies(remap_hbm, near, far, sems, FAR_SIZES, NEAR)
    slot_copy = pltpu.make_async_copy(slots_in, slots, sem)
    slot_copy.start()
    for copy in far_copies:
        copy.start()
    slot_copy.wait()
    for r in range(ROWS):
        rows[2 * r : 2 * r + 2, :] = returned[pl.ds(slots[r // 128, r % 128], 2), :]

    def four_rows(r, blocks):
        high, low = split(rows[2 * r : 2 * r + 8, :])
        left = jnp.concatenate([high, low], axis=0)
        four = lax.dot_general(
            left,
            blocks.reshape(4 * 128, 128),
            (((1,), (1,)), ((), ())),
            preferred_element_type=F32,
        )
        four = four[:8] + four[8:]
        for j in range(4):
            out[r + j] = four[2 * j : 2 * j + 2, j * 128 : (j + 1) * 128]

    out_copies = []

    def hand_on(start, size):
        part = pl.ds(start, size)
        copy = pltpu.make_async_copy(out.at[part], out_hbm.at[part], out_sems.at[len(out_copies)])
        copy.start()
        out_copies.append(copy)

    for r in range(0, NEAR, 4):
        four_rows(r, near[r : r + 4])
    hand_on(0, NEAR)
    for copy, (start, size) in zip(far_copies, spans(FAR_SIZES)):
        copy.wait()
        for r in range(start, start + size, 4):
            four_rows(NEAR + r, far[r : r + 4])
        hand_on(NEAR + start, size)
    for copy in out_copies:
        copy.wait()


def state(slots, returned, near, remap):
    return pl.pallas_call(
        state_kernel,
        out_shape=pltpu.HBM((ROWS, 2, 128), F32),
        in_specs=vmem_specs(3) + [pl.BlockSpec(memory_space=pltpu.HBM)],
        out_specs=pl.BlockSpec(memory_space=pltpu.HBM),
        scratch_shapes=[
            VMEM((ROWS - NEAR, 128, 128), BF16),
            VMEM((2 * ROWS, 128), F32),
            VMEM((ROWS, 2, 128), F32),
            SMEM((2, 128), jnp.int32),
            pltpu.SemaphoreType.DMA((len(FAR_SIZES),)),
            pltpu.SemaphoreType.DMA((len(FAR_SIZES) + 1,)),
            pltpu.SemaphoreType.DMA,
        ],
        compiler_params=params(20),
        cost_estimate=pl.CostEstimate(flops=10**9, bytes_accessed=9_000_000, transcendentals=0),
        name="state",
    )(slots, returned, near, remap)


def shifts(count, wraps):
    up = [(i, i + 1) for i in range(count - 1)] + ([(count - 1, 0)] if wraps else [])
    return up, [(b, a) for a, b in up]


def on_device(
    atmos_flux, remap_blocks, row_owner, row_target, tracers, east_vel, north_vel, mix_kappa, levels
):
    axes = ("lon", "lat")
    planes = tracers.reshape(2 * LEV, CY, CELLS)
    to_east, to_west, to_north, to_south = edges(planes, east_vel, north_vel, levels)
    eastward, westward = shifts(lax.axis_size("lon"), True)
    northward, southward = shifts(lax.axis_size("lat"), False)
    west_in = lax.ppermute(to_east, "lon", eastward)
    east_in = lax.ppermute(to_west, "lon", westward)
    south_in = lax.ppermute(to_north, "lat", northward)
    north_in = lax.ppermute(to_south, "lat", southward)
    send, slots, near = contributions(
        in_hbm(row_owner.reshape(2, 128)),
        in_hbm(row_target.reshape(2, 128)),
        in_hbm(jnp.transpose(atmos_flux, (1, 0, 2))),
        in_hbm(remap_blocks),
    )
    got = lax.all_to_all(
        send.reshape(DEV, BLOCK, 1, CELLS), axes, split_axis=0, concat_axis=0, tiled=True
    )
    inner = advected(planes, east_vel, north_vel, levels)
    after, answer = ocean(
        got.reshape(DEV * BLOCK, CELLS),
        inner,
        mix_kappa,
        levels,
        to_east,
        to_west,
        to_north,
        to_south,
        west_in,
        east_in,
        south_in,
        north_in,
    )
    returned = lax.all_to_all(answer, axes, split_axis=0, concat_axis=0, tiled=True)
    atmos_state = state(
        slots,
        returned.reshape(DEV * 2 * CAP, CELLS),
        pltpu.with_memory_space_constraint(near, VMEM),
        in_hbm(remap_blocks),
    )
    return after.reshape(2, LEV, CY, CELLS), atmos_state


def solution(mesh):
    row = ("lon", "lat")
    in_specs = (
        P(row, None, None),
        P(row, None, None),
        P(row, None),
        P(row),
        P(None, None, "lat", "lon"),
        P(None, "lat", "lon"),
        P(None, "lat", "lon"),
        P(None, "lat", "lon"),
        P("lat", "lon"),
    )
    out_specs = (P(None, None, "lat", "lon"), P(row, None, None))
    return jax.shard_map(
        on_device, mesh=mesh, in_specs=in_specs, out_specs=out_specs, check_vma=False
    )
```

```python
import math

import jax
import jax.numpy as jnp
from jax import lax
from jax.experimental import pallas as pl
from jax.experimental.pallas import tpu as pltpu
from jax.sharding import PartitionSpec as P

F32 = jnp.float32
BF16 = jnp.bfloat16

ROWS = 256
DEV = 128
CAP = 4
CELLS = 128
SENT = 4
BLOCK = CAP * SENT + 1
LEV = 8
CY = 32
CONTRIB_SIZES = (32, 48, 80, 96)
NEAR = 32
MID = 24
FAR_SIZES = (40, 64)
TURNED = 96
PIECE = 32

VMEM = pltpu.VMEM
SMEM = pltpu.SMEM


def split(x):
    high = x.astype(BF16)
    return high, (x - high.astype(F32)).astype(BF16)


def iota(shape, axis):
    return lax.broadcasted_iota(jnp.int32, shape, axis)


def spans(sizes):
    return [(sum(sizes[:i]), size) for i, size in enumerate(sizes)]


def block_copies(remap_hbm, near, far, sems, sizes, skipped=0):
    copies = []
    for i, (start, size) in enumerate(spans(sizes)):
        first = skipped + start
        inside = first < NEAR
        target = near.at[pl.ds(first, size)] if inside else far.at[pl.ds(first - NEAR, size)]
        copies.append(pltpu.make_async_copy(remap_hbm.at[pl.ds(first, size)], target, sems.at[i]))
    return copies


def in_hbm(x):
    return pltpu.with_memory_space_constraint(x, pltpu.HBM)


def params(mib):
    return pltpu.CompilerParams(vmem_limit_bytes=mib * 1024 * 1024)


def vmem_specs(count):
    return [pl.BlockSpec(memory_space=VMEM)] * count


def contrib_kernel(
    owner_hbm,
    target_hbm,
    flux_hbm,
    remap_hbm,
    send,
    slot_out,
    near,
    far,
    flux,
    fields,
    owner,
    target,
    slot_v,
    slot_s,
    sems,
    sem2,
):
    chunk_copies = block_copies(remap_hbm, near, far, sems, CONTRIB_SIZES)
    owner_copy = pltpu.make_async_copy(owner_hbm, owner, sem2.at[2])
    target_copy = pltpu.make_async_copy(target_hbm, target, sem2.at[3])
    flux_copy = pltpu.make_async_copy(flux_hbm, flux, sem2.at[0])
    owner_copy.start()
    target_copy.start()
    flux_copy.start()
    for copy in chunk_copies:
        copy.start()
    send[...] = jnp.zeros_like(send)
    owner_copy.wait()
    target_copy.wait()

    dev_iota = iota((DEV, 128), 0)
    own = owner[...]
    tgt = target[...].astype(F32) + 1.0
    member = jnp.concatenate(
        [(own[h : h + 1, :] == dev_iota).astype(F32) for h in range(2)], axis=1
    )
    before = (iota((ROWS, ROWS), 0) < iota((ROWS, ROWS), 1)).astype(BF16)
    earlier = jnp.dot(member.astype(BF16), before, preferred_element_type=F32)
    rank = jnp.sum(member * earlier, axis=0, keepdims=True)
    rank_i = rank.astype(jnp.int32)
    for h in range(2):
        slot_v[h : h + 1, :] = own[h : h + 1, :] * BLOCK + rank_i[:, h * 128 : (h + 1) * 128] * SENT
        slot_out[h : h + 1, :] = own[h : h + 1, :] * (2 * CAP) + rank_i[:, h * 128 : (h + 1) * 128] * 2
    slot_copy = pltpu.make_async_copy(slot_v, slot_s, sem2.at[1])
    slot_copy.start()
    tgt_row = jnp.concatenate([tgt[0:1, :], tgt[1:2, :]], axis=1)
    slot_tags = jnp.where(iota((DEV, ROWS), 0) == rank_i, tgt_row, 0.0).astype(BF16)
    tags = lax.dot_general(
        member.astype(BF16), slot_tags, (((1,), (1,)), ((), ())), preferred_element_type=F32
    )
    send[pl.ds(CAP * SENT, DEV, stride=BLOCK), :] = tags

    flux_copy.wait()
    fields[pl.ds(0, ROWS, stride=SENT), :] = flux[0]
    fields[pl.ds(1, ROWS, stride=SENT), :] = flux[1] + flux[2] + flux[3]
    fields[pl.ds(2, ROWS, stride=SENT), :] = flux[4]
    fields[pl.ds(3, ROWS, stride=SENT), :] = flux[5]
    slot_copy.wait()

    def pair(r):
        high, low = split(fields[pl.ds(pl.multiple_of(r * SENT, 8), 8), :])
        left = jnp.concatenate([high, low], axis=0)
        blocks = [near[i] if i < NEAR else far[i - NEAR] for i in (r, r + 1)]
        right = jnp.concatenate(blocks, axis=1)
        both = jnp.dot(left, right, preferred_element_type=F32)
        both = both[:8] + both[8:]
        first = slot_s[r // 128, r % 128]
        second = slot_s[(r + 1) // 128, (r + 1) % 128]
        send[pl.ds(first, SENT), :] = both[:4, :CELLS]
        send[pl.ds(second, SENT), :] = both[4:, CELLS:]

    for copy, (start, size) in zip(chunk_copies, spans(CONTRIB_SIZES)):
        copy.wait()
        for r in range(start, start + size, 2):
            pair(r)


def contributions(row_owner, row_target, flux, remap):
    return pl.pallas_call(
        contrib_kernel,
        out_shape=(
            jax.ShapeDtypeStruct((DEV * BLOCK, CELLS), F32),
            jax.ShapeDtypeStruct((2, 128), jnp.int32),
            VMEM((NEAR, 128, 128), BF16),
        ),
        in_specs=[pl.BlockSpec(memory_space=pltpu.HBM)] * 4,
        out_specs=tuple(vmem_specs(3)),
        scratch_shapes=[
            VMEM((ROWS - NEAR, 128, 128), BF16),
            VMEM((6, ROWS, 128), F32),
            VMEM((ROWS * SENT, 128), F32),
            VMEM((2, 128), jnp.int32),
            VMEM((2, 128), jnp.int32),
            VMEM((2, 128), jnp.int32),
            SMEM((2, 128), jnp.int32),
            pltpu.SemaphoreType.DMA((len(CONTRIB_SIZES),)),
            pltpu.SemaphoreType.DMA((4,)),
        ],
        compiler_params=params(24),
        cost_estimate=pl.CostEstimate(flops=10**9, bytes_accessed=10_000_000, transcendentals=0),
        name="contrib",
    )(row_owner, row_target, flux, remap)


def edge_kernel(tracers, east_vel, north_vel, levels, to_east, to_west, to_north, to_south):
    lev = levels[...].astype(F32)
    lane = iota((CY, 128), 1)
    zero = jnp.zeros((CY, 128), F32)
    east, west = zero, zero
    planes = [tracers[p] for p in range(16)] + [lev] + [east_vel[k] for k in range(LEV)]
    for p, plane in enumerate(planes):
        east = jnp.where(lane == p, pltpu.roll(plane, (p + 1) % 128, 1), east)
        if p < 17:
            west = jnp.where(lane == p, plane if p == 0 else pltpu.roll(plane, p, 1), west)
    to_east[...] = east
    to_west[...] = west
    to_north[...] = zero
    to_south[...] = zero
    for p in range(16):
        to_north[p : p + 1, :] = tracers[p, CY - 1 : CY, :]
        to_south[p : p + 1, :] = tracers[p, 0:1, :]
    to_north[16:17, :] = lev[CY - 1 : CY]
    to_south[16:17, :] = lev[0:1]
    for k in range(LEV):
        to_north[17 + k : 18 + k, :] = north_vel[k, CY - 1 : CY, :]


def edges(tracers, east_vel, north_vel, levels):
    return pl.pallas_call(
        edge_kernel,
        out_shape=tuple(jax.ShapeDtypeStruct((CY, 128), F32) for _ in range(4)),
        in_specs=vmem_specs(4),
        out_specs=tuple(vmem_specs(4)),
        compiler_params=params(8),
        cost_estimate=pl.CostEstimate(flops=10**5, bytes_accessed=1_000_000, transcendentals=0),
        name="edges",
    )(tracers, east_vel, north_vel, levels)


def advect_kernel(tracers, east_vel, north_vel, levels, out):
    lane_last = iota((CY, 128), 1) == 127
    row_last = iota((CY, 128), 0) == CY - 1
    lev = levels[...].astype(F32)
    lev_e = jnp.where(lane_last, 0.0, pltpu.roll(lev, 127, 1))
    lev_n = jnp.where(row_last, 0.0, pltpu.roll(lev, CY - 1, 0))
    for k in range(LEV):
        depth = float(k)
        wet = (lev > depth).astype(F32)
        wet_e = wet * (lev_e > depth).astype(F32)
        wet_n = wet * (lev_n > depth).astype(F32)
        vel_e, vel_n = east_vel[k], north_vel[k]
        e_pos, e_neg = jnp.maximum(vel_e, 0.0), jnp.minimum(vel_e, 0.0)
        n_pos, n_neg = jnp.maximum(vel_n, 0.0), jnp.minimum(vel_n, 0.0)
        for t in range(2):
            p = t * LEV + k
            here = tracers[p]
            flux_e = (e_pos * here + e_neg * pltpu.roll(here, 127, 1)) * wet_e
            flux_n = (n_pos * here + n_neg * pltpu.roll(here, CY - 1, 0)) * wet_n
            out[p] = here - (flux_e - pltpu.roll(flux_e, 1, 1)) - (flux_n - pltpu.roll(flux_n, 1, 0))


def advected(*args):
    return pl.pallas_call(
        advect_kernel,
        out_shape=jax.ShapeDtypeStruct((16, CY, 128), F32),
        in_specs=vmem_specs(4),
        out_specs=pl.BlockSpec(memory_space=VMEM),
        compiler_params=params(8),
        cost_estimate=pl.CostEstimate(flops=10**6, bytes_accessed=2_000_000, transcendentals=0),
        name="advect",
    )(*args)


def face(vel, low, high, lev_low, lev_high, depth):
    wet = (lev_low > depth).astype(F32) * (lev_high > depth).astype(F32)
    return (jnp.maximum(vel, 0.0) * low + jnp.minimum(vel, 0.0) * high) * wet


def side_face(low, high):
    lane = iota((CY, 128), 1)
    packed = low[...]
    vel = jnp.where(lane < LEV, pltpu.roll(packed, 128 - 17, 1), pltpu.roll(packed, 128 - 9, 1))
    return face(
        vel, packed, high[...], low[:, 16:17], high[:, 16:17], (lane % LEV).astype(F32)
    )


def end_face(low, high):
    vel = jnp.concatenate([low[17 : 17 + LEV, :]] * 2, axis=0)
    depth = (iota((2 * LEV, 128), 0) % LEV).astype(F32)
    return face(
        vel, low[0 : 2 * LEV, :], high[0 : 2 * LEV, :], low[16:17, :], high[16:17, :], depth
    )


def ocean_kernel(
    got,
    inner,
    kappa,
    levels,
    to_east,
    to_west,
    to_north,
    to_south,
    west_in,
    east_in,
    south_in,
    north_in,
    turned_hbm,
    after,
    answer,
):
    lane, row = iota((CY, 128), 1), iota((CY, 128), 0)
    from_west, to_next = side_face(west_in, to_west), side_face(to_east, east_in)
    from_south, to_top = end_face(south_in, to_south), end_face(to_north, north_in)
    carried = []
    for p in range(2 * LEV):
        west = from_west if p == 0 else pltpu.roll(from_west, 128 - p, 1)
        sides = jnp.where(lane == 0, west, 0.0)
        sides = jnp.where(lane == 127, -pltpu.roll(to_next, 127 - p, 1), sides)
        ends = jnp.where(row == 0, from_south[p : p + 1, :], 0.0)
        ends = jnp.where(row == CY - 1, -to_top[p : p + 1, :], ends)
        carried.append(inner[p] + sides + ends)
    tags = jnp.transpose(got[pl.ds(CAP * SENT, DEV, stride=BLOCK), :])
    labels = iota((CY, DEV), 0).astype(F32) + 1.0
    select = jnp.concatenate(
        [(tags[s : s + 1, :] == labels).astype(F32) for s in range(CAP)], axis=1
    ).astype(BF16)
    forcing = []
    for f in range(SENT):
        rows = jnp.concatenate(
            [got[pl.ds(s * SENT + f, DEV, stride=BLOCK), :] for s in range(CAP)], axis=0
        )
        high, low = split(rows)
        both = jnp.dot(select, jnp.concatenate([high, low], axis=1), preferred_element_type=F32)
        forcing.append(both[:, :CELLS] + both[:, CELLS:])
    short, surface_heat, fresh, wind = forcing
    lev = levels[...]
    stirring = 0.25 * wind * wind
    wet = [(lev > k).astype(F32) for k in range(LEV)]
    link = [None] + [
        (kappa[k] + stirring * math.exp(-0.5 * k)) * wet[k] for k in range(1, LEV)
    ]
    gains, offsets = [], []
    for k in range(LEV):
        fraction = math.exp(-0.5 * k) - math.exp(-0.5 * (k + 1))
        heat = wet[k] * (fraction * short)
        warmth, salt = carried[k] + heat, carried[LEV + k]
        if k == 0:
            warmth = warmth + 0.5 * wet[0] * surface_heat
            salt = salt + 0.5 * wet[0] * fresh
        diagonal = 1.0 if k == 0 else 1.0 + link[k]
        if k < LEV - 1:
            diagonal = diagonal + link[k + 1]
        if k > 0:
            diagonal = diagonal - link[k] * gains[-1]
            warmth = warmth + link[k] * offsets[-1][0]
            salt = salt + link[k] * offsets[-1][1]
        inverse = 1.0 / diagonal
        if k < LEV - 1:
            gains.append(link[k + 1] * inverse)
        offsets.append((warmth * inverse, salt * inverse))
    warmth, salt = offsets[-1]
    after[LEV - 1], after[2 * LEV - 1] = warmth, salt
    for k in range(LEV - 2, -1, -1):
        warmth = offsets[k][0] + gains[k] * warmth
        salt = offsets[k][1] + gains[k] * salt
        after[k], after[LEV + k] = warmth, salt
    high, low = split(jnp.concatenate([warmth, salt], axis=1))
    picked = lax.dot_general(
        select,
        jnp.concatenate([high, low], axis=1),
        (((0,), (0,)), ((), ())),
        preferred_element_type=F32,
    )
    for s in range(CAP):
        for f in range(2):
            rows = picked[s * DEV : (s + 1) * DEV]
            answer[:, 2 * s + f, :] = (
                rows[:, f * CELLS : (f + 1) * CELLS] + rows[:, (2 + f) * CELLS : (3 + f) * CELLS]
            )


def ocean(*args):
    return pl.pallas_call(
        ocean_kernel,
        out_shape=(
            jax.ShapeDtypeStruct((16, CY, 128), F32),
            jax.ShapeDtypeStruct((DEV, 2 * CAP, CELLS), F32),
        ),
        in_specs=vmem_specs(12) + [pl.BlockSpec(memory_space=pltpu.HBM)],
        out_specs=tuple(vmem_specs(2)),
        compiler_params=params(24),
        cost_estimate=pl.CostEstimate(flops=10**8, bytes_accessed=4_000_000, transcendentals=0),
        name="ocean",
    )(*args)


def turn_kernel(inner, remap_hbm, turned_hbm, mid, blocks, turned, mid_blocks, in_sems, out_sems):
    parts = [pl.ds(i * PIECE, PIECE) for i in range(TURNED // PIECE)]
    reads = [
        pltpu.make_async_copy(
            remap_hbm.at[pl.ds(ROWS - TURNED + i * PIECE, PIECE)], blocks.at[part], in_sems.at[i]
        )
        for i, part in enumerate(parts)
    ]
    writes = [
        pltpu.make_async_copy(turned.at[part], turned_hbm.at[part], out_sems.at[i])
        for i, part in enumerate(parts)
    ]
    mid_read = pltpu.make_async_copy(
        remap_hbm.at[pl.ds(NEAR, MID)], mid_blocks, in_sems.at[TURNED // PIECE]
    )
    for read in reads:
        read.start()
    mid_read.start()
    for i, (read, write) in enumerate(zip(reads, writes)):
        read.wait()
        for r in range(i * PIECE, (i + 1) * PIECE):
            turned[r] = blocks[r].T
        write.start()
    mid_read.wait()
    for r in range(MID):
        mid[r] = mid_blocks[r].T
    for write in writes:
        write.wait()


def turn(inner, remap):
    return pl.pallas_call(
        turn_kernel,
        out_shape=(pltpu.HBM((TURNED, 128, 128), BF16), VMEM((MID, 128, 128), BF16)),
        in_specs=vmem_specs(1) + [pl.BlockSpec(memory_space=pltpu.HBM)],
        out_specs=(pl.BlockSpec(memory_space=pltpu.HBM), pl.BlockSpec(memory_space=VMEM)),
        scratch_shapes=[
            VMEM((TURNED, 128, 128), BF16),
            VMEM((TURNED, 128, 128), BF16),
            VMEM((MID, 128, 128), BF16),
            pltpu.SemaphoreType.DMA((TURNED // PIECE + 1,)),
            pltpu.SemaphoreType.DMA((TURNED // PIECE,)),
        ],
        compiler_params=params(16),
        cost_estimate=pl.CostEstimate(flops=10**6, bytes_accessed=6_000_000, transcendentals=0),
        name="turn",
    )(inner, remap)


def state_kernel(slots_in, returned, near, mid, remap_hbm, turned_hbm, out_hbm, far, turned, rows, out, slots, sems, out_sems, sem):
    far_copies = block_copies(remap_hbm, near, far, sems, FAR_SIZES, NEAR + MID)
    slot_copy = pltpu.make_async_copy(slots_in, slots, sem)
    slot_copy.start()
    turned_copy = pltpu.make_async_copy(turned_hbm, turned, sems.at[len(FAR_SIZES)])
    for copy in far_copies:
        copy.start()
    turned_copy.start()
    slot_copy.wait()
    for r in range(ROWS):
        rows[2 * r : 2 * r + 2, :] = returned[pl.ds(slots[r // 128, r % 128], 2), :]

    def four_rows(r, blocks, transposed=False):
        high, low = split(rows[2 * r : 2 * r + 8, :])
        left = jnp.concatenate([high, low], axis=0)
        if transposed:
            right = jnp.concatenate([blocks[j] for j in range(4)], axis=1)
            four = jnp.dot(left, right, preferred_element_type=F32)
        else:
            four = lax.dot_general(
                left,
                blocks.reshape(4 * 128, 128),
                (((1,), (1,)), ((), ())),
                preferred_element_type=F32,
            )
        four = four[:8] + four[8:]
        for j in range(4):
            out[r + j] = four[2 * j : 2 * j + 2, j * 128 : (j + 1) * 128]

    out_copies = []

    def hand_on(start, size):
        part = pl.ds(start, size)
        copy = pltpu.make_async_copy(out.at[part], out_hbm.at[part], out_sems.at[len(out_copies)])
        copy.start()
        out_copies.append(copy)

    for r in range(0, NEAR, 4):
        four_rows(r, near[r : r + 4])
    for r in range(0, MID, 4):
        four_rows(NEAR + r, mid[r : r + 4], True)
    hand_on(0, NEAR + MID)
    for copy, (start, size) in zip(far_copies, spans(FAR_SIZES)):
        copy.wait()
        for r in range(MID + start, MID + start + size, 4):
            four_rows(NEAR + r, far[r : r + 4])
        hand_on(NEAR + MID + start, size)
    turned_copy.wait()
    for r in range(0, TURNED, 4):
        four_rows(ROWS - TURNED + r, turned[r : r + 4], True)
    hand_on(ROWS - TURNED, TURNED)
    for copy in out_copies:
        copy.wait()


def state(slots, returned, near, mid, remap, turned):
    return pl.pallas_call(
        state_kernel,
        out_shape=pltpu.HBM((ROWS, 2, 128), F32),
        in_specs=vmem_specs(4) + [pl.BlockSpec(memory_space=pltpu.HBM)] * 2,
        out_specs=pl.BlockSpec(memory_space=pltpu.HBM),
        scratch_shapes=[
            VMEM((ROWS - NEAR - TURNED, 128, 128), BF16),
            VMEM((TURNED, 128, 128), BF16),
            VMEM((2 * ROWS, 128), F32),
            VMEM((ROWS, 2, 128), F32),
            SMEM((2, 128), jnp.int32),
            pltpu.SemaphoreType.DMA((len(FAR_SIZES) + 1,)),
            pltpu.SemaphoreType.DMA((len(FAR_SIZES) + 2,)),
            pltpu.SemaphoreType.DMA,
        ],
        compiler_params=params(20),
        cost_estimate=pl.CostEstimate(flops=10**9, bytes_accessed=9_000_000, transcendentals=0),
        name="state",
    )(slots, returned, near, mid, remap, turned)


def shifts(count, wraps):
    up = [(i, i + 1) for i in range(count - 1)] + ([(count - 1, 0)] if wraps else [])
    return up, [(b, a) for a, b in up]


def on_device(
    atmos_flux, remap_blocks, row_owner, row_target, tracers, east_vel, north_vel, mix_kappa, levels
):
    axes = ("lon", "lat")
    planes = tracers.reshape(2 * LEV, CY, CELLS)
    to_east, to_west, to_north, to_south = edges(planes, east_vel, north_vel, levels)
    eastward, westward = shifts(lax.axis_size("lon"), True)
    northward, southward = shifts(lax.axis_size("lat"), False)
    west_in = lax.ppermute(to_east, "lon", eastward)
    east_in = lax.ppermute(to_west, "lon", westward)
    south_in = lax.ppermute(to_north, "lat", northward)
    north_in = lax.ppermute(to_south, "lat", southward)
    send, slots, near = contributions(
        in_hbm(row_owner.reshape(2, 128)),
        in_hbm(row_target.reshape(2, 128)),
        in_hbm(jnp.transpose(atmos_flux, (1, 0, 2))),
        in_hbm(remap_blocks),
    )
    got = lax.all_to_all(
        send.reshape(DEV, BLOCK, 1, CELLS), axes, split_axis=0, concat_axis=0, tiled=True
    )
    inner = advected(planes, east_vel, north_vel, levels)
    turned, mid = turn(inner, in_hbm(remap_blocks))
    after, answer = ocean(
        got.reshape(DEV * BLOCK, CELLS),
        inner,
        mix_kappa,
        levels,
        to_east,
        to_west,
        to_north,
        to_south,
        west_in,
        east_in,
        south_in,
        north_in,
        in_hbm(turned),
    )
    returned = lax.all_to_all(answer, axes, split_axis=0, concat_axis=0, tiled=True)
    atmos_state = state(
        slots,
        returned.reshape(DEV * 2 * CAP, CELLS),
        pltpu.with_memory_space_constraint(near, VMEM),
        pltpu.with_memory_space_constraint(mid, VMEM),
        in_hbm(remap_blocks),
        in_hbm(turned),
    )
    return after.reshape(2, LEV, CY, CELLS), atmos_state


def solution(mesh):
    row = ("lon", "lat")
    in_specs = (
        P(row, None, None),
        P(row, None, None),
        P(row, None),
        P(row),
        P(None, None, "lat", "lon"),
        P(None, "lat", "lon"),
        P(None, "lat", "lon"),
        P(None, "lat", "lon"),
        P("lat", "lon"),
    )
    out_specs = (P(None, None, "lat", "lon"), P(row, None, None))
    return jax.shard_map(
        on_device, mesh=mesh, in_specs=in_specs, out_specs=out_specs, check_vma=False
    )
```

```python
import math

import jax
import jax.numpy as jnp
from jax import lax
from jax.experimental import pallas as pl
from jax.experimental.pallas import tpu as pltpu
from jax.sharding import PartitionSpec as P

F32 = jnp.float32
BF16 = jnp.bfloat16

ROWS = 256
DEV = 128
CAP = 4
CELLS = 128
SENT = 4
BLOCK = CAP * SENT + 1
LEV = 8
CY = 32
CONTRIB_SIZES = (32, 128, 96)
NEAR = 32
MID = 24
FAR_SIZES = (40, 64)
TURNED = 96
PIECE = 32

VMEM = pltpu.VMEM
SMEM = pltpu.SMEM


def split(x):
    high = x.astype(BF16)
    return high, (x - high.astype(F32)).astype(BF16)


def iota(shape, axis):
    return lax.broadcasted_iota(jnp.int32, shape, axis)


def spans(sizes):
    return [(sum(sizes[:i]), size) for i, size in enumerate(sizes)]


def block_copies(remap_hbm, near, far, sems, sizes, skipped=0):
    copies = []
    for i, (start, size) in enumerate(spans(sizes)):
        first = skipped + start
        inside = first < NEAR
        target = near.at[pl.ds(first, size)] if inside else far.at[pl.ds(first - NEAR, size)]
        copies.append(pltpu.make_async_copy(remap_hbm.at[pl.ds(first, size)], target, sems.at[i]))
    return copies


def in_hbm(x):
    return pltpu.with_memory_space_constraint(x, pltpu.HBM)


def params(mib):
    return pltpu.CompilerParams(vmem_limit_bytes=mib * 1024 * 1024)


def vmem_specs(count):
    return [pl.BlockSpec(memory_space=VMEM)] * count


def contrib_kernel(
    owner_hbm,
    target_hbm,
    flux_hbm,
    remap_hbm,
    send,
    slot_out,
    near,
    far,
    flux,
    fields,
    owner,
    target,
    slot_v,
    slot_s,
    sems,
    sem2,
):
    chunk_copies = block_copies(remap_hbm, near, far, sems, CONTRIB_SIZES)
    owner_copy = pltpu.make_async_copy(owner_hbm, owner, sem2.at[2])
    target_copy = pltpu.make_async_copy(target_hbm, target, sem2.at[3])
    flux_copy = pltpu.make_async_copy(flux_hbm, flux, sem2.at[0])
    owner_copy.start()
    target_copy.start()
    flux_copy.start()
    for copy in chunk_copies:
        copy.start()
    send[...] = jnp.zeros_like(send)
    owner_copy.wait()
    target_copy.wait()

    dev_iota = iota((DEV, 128), 0)
    own = owner[...]
    tgt = target[...].astype(F32) + 1.0
    member = jnp.concatenate(
        [(own[h : h + 1, :] == dev_iota).astype(F32) for h in range(2)], axis=1
    )
    before = (iota((ROWS, ROWS), 0) < iota((ROWS, ROWS), 1)).astype(BF16)
    earlier = jnp.dot(member.astype(BF16), before, preferred_element_type=F32)
    rank = jnp.sum(member * earlier, axis=0, keepdims=True)
    rank_i = rank.astype(jnp.int32)
    for h in range(2):
        slot_v[h : h + 1, :] = own[h : h + 1, :] * BLOCK + rank_i[:, h * 128 : (h + 1) * 128] * SENT
        slot_out[h : h + 1, :] = own[h : h + 1, :] * (2 * CAP) + rank_i[:, h * 128 : (h + 1) * 128] * 2
    slot_copy = pltpu.make_async_copy(slot_v, slot_s, sem2.at[1])
    slot_copy.start()
    tgt_row = jnp.concatenate([tgt[0:1, :], tgt[1:2, :]], axis=1)
    slot_tags = jnp.where(iota((DEV, ROWS), 0) == rank_i, tgt_row, 0.0).astype(BF16)
    tags = lax.dot_general(
        member.astype(BF16), slot_tags, (((1,), (1,)), ((), ())), preferred_element_type=F32
    )
    send[pl.ds(CAP * SENT, DEV, stride=BLOCK), :] = tags

    flux_copy.wait()
    fields[pl.ds(0, ROWS, stride=SENT), :] = flux[0]
    fields[pl.ds(1, ROWS, stride=SENT), :] = flux[1] + flux[2] + flux[3]
    fields[pl.ds(2, ROWS, stride=SENT), :] = flux[4]
    fields[pl.ds(3, ROWS, stride=SENT), :] = flux[5]
    slot_copy.wait()

    def pair(r):
        high, low = split(fields[pl.ds(pl.multiple_of(r * SENT, 8), 8), :])
        left = jnp.concatenate([high, low], axis=0)
        blocks = [near[i] if i < NEAR else far[i - NEAR] for i in (r, r + 1)]
        right = jnp.concatenate(blocks, axis=1)
        both = jnp.dot(left, right, preferred_element_type=F32)
        both = both[:8] + both[8:]
        first = slot_s[r // 128, r % 128]
        second = slot_s[(r + 1) // 128, (r + 1) % 128]
        send[pl.ds(first, SENT), :] = both[:4, :CELLS]
        send[pl.ds(second, SENT), :] = both[4:, CELLS:]

    for copy, (start, size) in zip(chunk_copies, spans(CONTRIB_SIZES)):
        copy.wait()
        for r in range(start, start + size, 2):
            pair(r)


def contributions(row_owner, row_target, flux, remap):
    return pl.pallas_call(
        contrib_kernel,
        out_shape=(
            jax.ShapeDtypeStruct((DEV * BLOCK, CELLS), F32),
            jax.ShapeDtypeStruct((2, 128), jnp.int32),
            VMEM((NEAR, 128, 128), BF16),
        ),
        in_specs=[pl.BlockSpec(memory_space=pltpu.HBM)] * 4,
        out_specs=tuple(vmem_specs(3)),
        scratch_shapes=[
            VMEM((ROWS - NEAR, 128, 128), BF16),
            VMEM((6, ROWS, 128), F32),
            VMEM((ROWS * SENT, 128), F32),
            VMEM((2, 128), jnp.int32),
            VMEM((2, 128), jnp.int32),
            VMEM((2, 128), jnp.int32),
            SMEM((2, 128), jnp.int32),
            pltpu.SemaphoreType.DMA((len(CONTRIB_SIZES),)),
            pltpu.SemaphoreType.DMA((4,)),
        ],
        compiler_params=params(24),
        cost_estimate=pl.CostEstimate(flops=10**9, bytes_accessed=10_000_000, transcendentals=0),
        name="contrib",
    )(row_owner, row_target, flux, remap)


def edge_kernel(tracers, east_vel, north_vel, levels, to_east, to_west, to_north, to_south):
    lev = levels[...].astype(F32)
    lane = iota((CY, 128), 1)
    zero = jnp.zeros((CY, 128), F32)
    east, west = zero, zero
    planes = [tracers[p] for p in range(16)] + [lev] + [east_vel[k] for k in range(LEV)]
    for p, plane in enumerate(planes):
        east = jnp.where(lane == p, pltpu.roll(plane, (p + 1) % 128, 1), east)
        if p < 17:
            west = jnp.where(lane == p, plane if p == 0 else pltpu.roll(plane, p, 1), west)
    to_east[...] = east
    to_west[...] = west
    to_north[...] = zero
    to_south[...] = zero
    for p in range(16):
        to_north[p : p + 1, :] = tracers[p, CY - 1 : CY, :]
        to_south[p : p + 1, :] = tracers[p, 0:1, :]
    to_north[16:17, :] = lev[CY - 1 : CY]
    to_south[16:17, :] = lev[0:1]
    for k in range(LEV):
        to_north[17 + k : 18 + k, :] = north_vel[k, CY - 1 : CY, :]


def edges(tracers, east_vel, north_vel, levels):
    return pl.pallas_call(
        edge_kernel,
        out_shape=tuple(jax.ShapeDtypeStruct((CY, 128), F32) for _ in range(4)),
        in_specs=vmem_specs(4),
        out_specs=tuple(vmem_specs(4)),
        compiler_params=params(8),
        cost_estimate=pl.CostEstimate(flops=10**5, bytes_accessed=1_000_000, transcendentals=0),
        name="edges",
    )(tracers, east_vel, north_vel, levels)


def advect_kernel(tracers, east_vel, north_vel, levels, out):
    lane_last = iota((CY, 128), 1) == 127
    row_last = iota((CY, 128), 0) == CY - 1
    lev = levels[...].astype(F32)
    lev_e = jnp.where(lane_last, 0.0, pltpu.roll(lev, 127, 1))
    lev_n = jnp.where(row_last, 0.0, pltpu.roll(lev, CY - 1, 0))
    for k in range(LEV):
        depth = float(k)
        wet = (lev > depth).astype(F32)
        wet_e = wet * (lev_e > depth).astype(F32)
        wet_n = wet * (lev_n > depth).astype(F32)
        vel_e, vel_n = east_vel[k], north_vel[k]
        e_pos, e_neg = jnp.maximum(vel_e, 0.0), jnp.minimum(vel_e, 0.0)
        n_pos, n_neg = jnp.maximum(vel_n, 0.0), jnp.minimum(vel_n, 0.0)
        for t in range(2):
            p = t * LEV + k
            here = tracers[p]
            flux_e = (e_pos * here + e_neg * pltpu.roll(here, 127, 1)) * wet_e
            flux_n = (n_pos * here + n_neg * pltpu.roll(here, CY - 1, 0)) * wet_n
            out[p] = here - (flux_e - pltpu.roll(flux_e, 1, 1)) - (flux_n - pltpu.roll(flux_n, 1, 0))


def advected(*args):
    return pl.pallas_call(
        advect_kernel,
        out_shape=jax.ShapeDtypeStruct((16, CY, 128), F32),
        in_specs=vmem_specs(4),
        out_specs=pl.BlockSpec(memory_space=VMEM),
        compiler_params=params(8),
        cost_estimate=pl.CostEstimate(flops=10**6, bytes_accessed=2_000_000, transcendentals=0),
        name="advect",
    )(*args)


def face(vel, low, high, lev_low, lev_high, depth):
    wet = (lev_low > depth).astype(F32) * (lev_high > depth).astype(F32)
    return (jnp.maximum(vel, 0.0) * low + jnp.minimum(vel, 0.0) * high) * wet


def side_face(low, high):
    lane = iota((CY, 128), 1)
    packed = low[...]
    vel = jnp.where(lane < LEV, pltpu.roll(packed, 128 - 17, 1), pltpu.roll(packed, 128 - 9, 1))
    return face(
        vel, packed, high[...], low[:, 16:17], high[:, 16:17], (lane % LEV).astype(F32)
    )


def end_face(low, high):
    vel = jnp.concatenate([low[17 : 17 + LEV, :]] * 2, axis=0)
    depth = (iota((2 * LEV, 128), 0) % LEV).astype(F32)
    return face(
        vel, low[0 : 2 * LEV, :], high[0 : 2 * LEV, :], low[16:17, :], high[16:17, :], depth
    )


def ocean_kernel(
    got,
    inner,
    kappa,
    levels,
    to_east,
    to_west,
    to_north,
    to_south,
    west_in,
    east_in,
    south_in,
    north_in,
    turned_hbm,
    after_hbm,
    answer,
    after,
    sem,
):
    lane, row = iota((CY, 128), 1), iota((CY, 128), 0)
    from_west, to_next = side_face(west_in, to_west), side_face(to_east, east_in)
    from_south, to_top = end_face(south_in, to_south), end_face(to_north, north_in)
    carried = []
    for p in range(2 * LEV):
        west = from_west if p == 0 else pltpu.roll(from_west, 128 - p, 1)
        sides = jnp.where(lane == 0, west, 0.0)
        sides = jnp.where(lane == 127, -pltpu.roll(to_next, 127 - p, 1), sides)
        ends = jnp.where(row == 0, from_south[p : p + 1, :], 0.0)
        ends = jnp.where(row == CY - 1, -to_top[p : p + 1, :], ends)
        carried.append(inner[p] + sides + ends)
    tags = jnp.transpose(got[pl.ds(CAP * SENT, DEV, stride=BLOCK), :])
    labels = iota((CY, DEV), 0).astype(F32) + 1.0
    select = jnp.concatenate(
        [(tags[s : s + 1, :] == labels).astype(F32) for s in range(CAP)], axis=1
    ).astype(BF16)
    forcing = []
    for f in range(SENT):
        rows = jnp.concatenate(
            [got[pl.ds(s * SENT + f, DEV, stride=BLOCK), :] for s in range(CAP)], axis=0
        )
        high, low = split(rows)
        both = jnp.dot(select, jnp.concatenate([high, low], axis=1), preferred_element_type=F32)
        forcing.append(both[:, :CELLS] + both[:, CELLS:])
    short, surface_heat, fresh, wind = forcing
    lev = levels[...]
    stirring = 0.25 * wind * wind
    wet = [(lev > k).astype(F32) for k in range(LEV)]
    link = [None] + [
        (kappa[k] + stirring * math.exp(-0.5 * k)) * wet[k] for k in range(1, LEV)
    ]
    gains, offsets = [], []
    for k in range(LEV):
        fraction = math.exp(-0.5 * k) - math.exp(-0.5 * (k + 1))
        heat = wet[k] * (fraction * short)
        warmth, salt = carried[k] + heat, carried[LEV + k]
        if k == 0:
            warmth = warmth + 0.5 * wet[0] * surface_heat
            salt = salt + 0.5 * wet[0] * fresh
        diagonal = 1.0 if k == 0 else 1.0 + link[k]
        if k < LEV - 1:
            diagonal = diagonal + link[k + 1]
        if k > 0:
            diagonal = diagonal - link[k] * gains[-1]
            warmth = warmth + link[k] * offsets[-1][0]
            salt = salt + link[k] * offsets[-1][1]
        inverse = 1.0 / diagonal
        if k < LEV - 1:
            gains.append(link[k + 1] * inverse)
        offsets.append((warmth * inverse, salt * inverse))
    warmth, salt = offsets[-1]
    after[LEV - 1], after[2 * LEV - 1] = warmth, salt
    for k in range(LEV - 2, -1, -1):
        warmth = offsets[k][0] + gains[k] * warmth
        salt = offsets[k][1] + gains[k] * salt
        after[k], after[LEV + k] = warmth, salt
    after_copy = pltpu.make_async_copy(after, after_hbm, sem)
    after_copy.start()
    high, low = split(jnp.concatenate([warmth, salt], axis=1))
    picked = lax.dot_general(
        select,
        jnp.concatenate([high, low], axis=1),
        (((0,), (0,)), ((), ())),
        preferred_element_type=F32,
    )
    for s in range(CAP):
        for f in range(2):
            rows = picked[s * DEV : (s + 1) * DEV]
            answer[:, 2 * s + f, :] = (
                rows[:, f * CELLS : (f + 1) * CELLS] + rows[:, (2 + f) * CELLS : (3 + f) * CELLS]
            )
    after_copy.wait()


def ocean(*args):
    return pl.pallas_call(
        ocean_kernel,
        out_shape=(
            pltpu.HBM((16, CY, 128), F32),
            jax.ShapeDtypeStruct((DEV, 2 * CAP, CELLS), F32),
        ),
        in_specs=vmem_specs(12) + [pl.BlockSpec(memory_space=pltpu.HBM)],
        out_specs=(pl.BlockSpec(memory_space=pltpu.HBM), pl.BlockSpec(memory_space=VMEM)),
        scratch_shapes=[VMEM((16, CY, 128), F32), pltpu.SemaphoreType.DMA],
        compiler_params=params(24),
        cost_estimate=pl.CostEstimate(flops=10**8, bytes_accessed=4_000_000, transcendentals=0),
        name="ocean",
    )(*args)


def turn_kernel(inner, remap_hbm, turned_hbm, mid, blocks, turned, mid_blocks, in_sems, out_sems):
    parts = [pl.ds(i * PIECE, PIECE) for i in range(TURNED // PIECE)]
    reads = [
        pltpu.make_async_copy(
            remap_hbm.at[pl.ds(ROWS - TURNED + i * PIECE, PIECE)], blocks.at[part], in_sems.at[i]
        )
        for i, part in enumerate(parts)
    ]
    writes = [
        pltpu.make_async_copy(turned.at[part], turned_hbm.at[part], out_sems.at[i])
        for i, part in enumerate(parts)
    ]
    mid_read = pltpu.make_async_copy(
        remap_hbm.at[pl.ds(NEAR, MID)], mid_blocks, in_sems.at[TURNED // PIECE]
    )
    for read in reads:
        read.start()
    mid_read.start()
    for i, (read, write) in enumerate(zip(reads, writes)):
        read.wait()
        for r in range(i * PIECE, (i + 1) * PIECE):
            turned[r] = blocks[r].T
        write.start()
    mid_read.wait()
    for r in range(MID):
        mid[r] = mid_blocks[r].T
    for write in writes:
        write.wait()


def turn(inner, remap):
    return pl.pallas_call(
        turn_kernel,
        out_shape=(pltpu.HBM((TURNED, 128, 128), BF16), VMEM((MID, 128, 128), BF16)),
        in_specs=vmem_specs(1) + [pl.BlockSpec(memory_space=pltpu.HBM)],
        out_specs=(pl.BlockSpec(memory_space=pltpu.HBM), pl.BlockSpec(memory_space=VMEM)),
        scratch_shapes=[
            VMEM((TURNED, 128, 128), BF16),
            VMEM((TURNED, 128, 128), BF16),
            VMEM((MID, 128, 128), BF16),
            pltpu.SemaphoreType.DMA((TURNED // PIECE + 1,)),
            pltpu.SemaphoreType.DMA((TURNED // PIECE,)),
        ],
        compiler_params=params(16),
        cost_estimate=pl.CostEstimate(flops=10**6, bytes_accessed=6_000_000, transcendentals=0),
        name="turn",
    )(inner, remap)


def state_kernel(slots_in, returned, near, mid, remap_hbm, turned_hbm, out_hbm, far, turned, rows, out, slots, sems, out_sems, sem):
    far_copies = block_copies(remap_hbm, near, far, sems, FAR_SIZES, NEAR + MID)
    slot_copy = pltpu.make_async_copy(slots_in, slots, sem)
    slot_copy.start()
    turned_copy = pltpu.make_async_copy(turned_hbm, turned, sems.at[len(FAR_SIZES)])
    for copy in far_copies:
        copy.start()
    turned_copy.start()
    slot_copy.wait()
    for r in range(ROWS):
        rows[2 * r : 2 * r + 2, :] = returned[pl.ds(slots[r // 128, r % 128], 2), :]

    def four_rows(r, blocks, transposed=False):
        high, low = split(rows[2 * r : 2 * r + 8, :])
        left = jnp.concatenate([high, low], axis=0)
        if transposed:
            right = jnp.concatenate([blocks[j] for j in range(4)], axis=1)
            four = jnp.dot(left, right, preferred_element_type=F32)
        else:
            four = lax.dot_general(
                left,
                blocks.reshape(4 * 128, 128),
                (((1,), (1,)), ((), ())),
                preferred_element_type=F32,
            )
        four = four[:8] + four[8:]
        for j in range(4):
            out[r + j] = four[2 * j : 2 * j + 2, j * 128 : (j + 1) * 128]

    out_copies = []

    def hand_on(start, size):
        part = pl.ds(start, size)
        copy = pltpu.make_async_copy(out.at[part], out_hbm.at[part], out_sems.at[len(out_copies)])
        copy.start()
        out_copies.append(copy)

    for r in range(0, NEAR, 4):
        four_rows(r, near[r : r + 4])
    for r in range(0, MID, 4):
        four_rows(NEAR + r, mid[r : r + 4], True)
    hand_on(0, NEAR + MID)
    for copy, (start, size) in zip(far_copies, spans(FAR_SIZES)):
        copy.wait()
        for r in range(MID + start, MID + start + size, 4):
            four_rows(NEAR + r, far[r : r + 4])
        hand_on(NEAR + MID + start, size)
    turned_copy.wait()
    for r in range(0, TURNED, 4):
        four_rows(ROWS - TURNED + r, turned[r : r + 4], True)
    hand_on(ROWS - TURNED, TURNED)
    for copy in out_copies:
        copy.wait()


def state(slots, returned, near, mid, remap, turned):
    return pl.pallas_call(
        state_kernel,
        out_shape=pltpu.HBM((ROWS, 2, 128), F32),
        in_specs=vmem_specs(4) + [pl.BlockSpec(memory_space=pltpu.HBM)] * 2,
        out_specs=pl.BlockSpec(memory_space=pltpu.HBM),
        scratch_shapes=[
            VMEM((ROWS - NEAR - TURNED, 128, 128), BF16),
            VMEM((TURNED, 128, 128), BF16),
            VMEM((2 * ROWS, 128), F32),
            VMEM((ROWS, 2, 128), F32),
            SMEM((2, 128), jnp.int32),
            pltpu.SemaphoreType.DMA((len(FAR_SIZES) + 1,)),
            pltpu.SemaphoreType.DMA((len(FAR_SIZES) + 2,)),
            pltpu.SemaphoreType.DMA,
        ],
        compiler_params=params(20),
        cost_estimate=pl.CostEstimate(flops=10**9, bytes_accessed=9_000_000, transcendentals=0),
        name="state",
    )(slots, returned, near, mid, remap, turned)


def shifts(count, wraps):
    up = [(i, i + 1) for i in range(count - 1)] + ([(count - 1, 0)] if wraps else [])
    return up, [(b, a) for a, b in up]


def on_device(
    atmos_flux, remap_blocks, row_owner, row_target, tracers, east_vel, north_vel, mix_kappa, levels
):
    axes = ("lon", "lat")
    planes = tracers.reshape(2 * LEV, CY, CELLS)
    to_east, to_west, to_north, to_south = edges(planes, east_vel, north_vel, levels)
    eastward, westward = shifts(lax.axis_size("lon"), True)
    northward, southward = shifts(lax.axis_size("lat"), False)
    west_in = lax.ppermute(to_east, "lon", eastward)
    east_in = lax.ppermute(to_west, "lon", westward)
    south_in = lax.ppermute(to_north, "lat", northward)
    north_in = lax.ppermute(to_south, "lat", southward)
    send, slots, near = contributions(
        in_hbm(row_owner.reshape(2, 128)),
        in_hbm(row_target.reshape(2, 128)),
        in_hbm(jnp.transpose(atmos_flux, (1, 0, 2))),
        in_hbm(remap_blocks),
    )
    got = lax.all_to_all(
        send.reshape(DEV, BLOCK, 1, CELLS), axes, split_axis=0, concat_axis=0, tiled=True
    )
    inner = advected(planes, east_vel, north_vel, levels)
    turned, mid = turn(inner, in_hbm(remap_blocks))
    after, answer = ocean(
        got.reshape(DEV * BLOCK, CELLS),
        inner,
        mix_kappa,
        levels,
        to_east,
        to_west,
        to_north,
        to_south,
        west_in,
        east_in,
        south_in,
        north_in,
        in_hbm(turned),
    )
    returned = lax.all_to_all(answer, axes, split_axis=0, concat_axis=0, tiled=True)
    atmos_state = state(
        slots,
        returned.reshape(DEV * 2 * CAP, CELLS),
        pltpu.with_memory_space_constraint(near, VMEM),
        pltpu.with_memory_space_constraint(mid, VMEM),
        in_hbm(remap_blocks),
        in_hbm(turned),
    )
    return after.reshape(2, LEV, CY, CELLS), atmos_state


def solution(mesh):
    row = ("lon", "lat")
    in_specs = (
        P(row, None, None),
        P(row, None, None),
        P(row, None),
        P(row),
        P(None, None, "lat", "lon"),
        P(None, "lat", "lon"),
        P(None, "lat", "lon"),
        P(None, "lat", "lon"),
        P("lat", "lon"),
    )
    out_specs = (P(None, None, "lat", "lon"), P(row, None, None))
    return jax.shard_map(
        on_device, mesh=mesh, in_specs=in_specs, out_specs=out_specs, check_vma=False
    )
```

```python
import math

import jax
import jax.numpy as jnp
from jax import lax
from jax.experimental import pallas as pl
from jax.experimental.pallas import tpu as pltpu
from jax.sharding import PartitionSpec as P

F32 = jnp.float32
BF16 = jnp.bfloat16

ROWS = 256
DEV = 128
CAP = 4
CELLS = 128
SENT = 4
BLOCK = CAP * SENT + 1
LEV = 8
CY = 32
CONTRIB_SIZES = (32, 128, 96)
NEAR = 32
MID = 24
FAR_SIZES = (104,)
TURNED = 96
PIECE = 32

VMEM = pltpu.VMEM
SMEM = pltpu.SMEM


def split(x):
    high = x.astype(BF16)
    return high, (x - high.astype(F32)).astype(BF16)


def iota(shape, axis):
    return lax.broadcasted_iota(jnp.int32, shape, axis)


def spans(sizes):
    return [(sum(sizes[:i]), size) for i, size in enumerate(sizes)]


def block_copies(remap_hbm, near, far, sems, sizes, skipped=0):
    copies = []
    for i, (start, size) in enumerate(spans(sizes)):
        first = skipped + start
        inside = first < NEAR
        target = near.at[pl.ds(first, size)] if inside else far.at[pl.ds(first - NEAR, size)]
        copies.append(pltpu.make_async_copy(remap_hbm.at[pl.ds(first, size)], target, sems.at[i]))
    return copies


def in_hbm(x):
    return pltpu.with_memory_space_constraint(x, pltpu.HBM)


def params(mib):
    return pltpu.CompilerParams(vmem_limit_bytes=mib * 1024 * 1024)


def vmem_specs(count):
    return [pl.BlockSpec(memory_space=VMEM)] * count


def contrib_kernel(
    owner_hbm,
    target_hbm,
    flux_hbm,
    remap_hbm,
    send,
    slot_out,
    near,
    far,
    flux,
    fields,
    owner,
    target,
    slot_v,
    slot_s,
    sems,
    sem2,
):
    chunk_copies = block_copies(remap_hbm, near, far, sems, CONTRIB_SIZES)
    owner_copy = pltpu.make_async_copy(owner_hbm, owner, sem2.at[2])
    target_copy = pltpu.make_async_copy(target_hbm, target, sem2.at[3])
    flux_copy = pltpu.make_async_copy(flux_hbm, flux, sem2.at[0])
    owner_copy.start()
    target_copy.start()
    flux_copy.start()
    for copy in chunk_copies:
        copy.start()
    send[...] = jnp.zeros_like(send)
    owner_copy.wait()
    target_copy.wait()

    dev_iota = iota((DEV, 128), 0)
    own = owner[...]
    tgt = target[...].astype(F32) + 1.0
    member = jnp.concatenate(
        [(own[h : h + 1, :] == dev_iota).astype(F32) for h in range(2)], axis=1
    )
    before = (iota((ROWS, ROWS), 0) < iota((ROWS, ROWS), 1)).astype(BF16)
    earlier = jnp.dot(member.astype(BF16), before, preferred_element_type=F32)
    rank = jnp.sum(member * earlier, axis=0, keepdims=True)
    rank_i = rank.astype(jnp.int32)
    for h in range(2):
        slot_v[h : h + 1, :] = own[h : h + 1, :] * BLOCK + rank_i[:, h * 128 : (h + 1) * 128] * SENT
        slot_out[h : h + 1, :] = own[h : h + 1, :] * (2 * CAP) + rank_i[:, h * 128 : (h + 1) * 128] * 2
    slot_copy = pltpu.make_async_copy(slot_v, slot_s, sem2.at[1])
    slot_copy.start()
    tgt_row = jnp.concatenate([tgt[0:1, :], tgt[1:2, :]], axis=1)
    slot_tags = jnp.where(iota((DEV, ROWS), 0) == rank_i, tgt_row, 0.0).astype(BF16)
    tags = lax.dot_general(
        member.astype(BF16), slot_tags, (((1,), (1,)), ((), ())), preferred_element_type=F32
    )
    send[pl.ds(CAP * SENT, DEV, stride=BLOCK), :] = tags

    flux_copy.wait()
    fields[pl.ds(0, ROWS, stride=SENT), :] = flux[0]
    fields[pl.ds(1, ROWS, stride=SENT), :] = flux[1] + flux[2] + flux[3]
    fields[pl.ds(2, ROWS, stride=SENT), :] = flux[4]
    fields[pl.ds(3, ROWS, stride=SENT), :] = flux[5]
    slot_copy.wait()

    def pair(r):
        high, low = split(fields[pl.ds(pl.multiple_of(r * SENT, 8), 8), :])
        left = jnp.concatenate([high, low], axis=0)
        blocks = [near[i] if i < NEAR else far[i - NEAR] for i in (r, r + 1)]
        right = jnp.concatenate(blocks, axis=1)
        both = jnp.dot(left, right, preferred_element_type=F32)
        both = both[:8] + both[8:]
        first = slot_s[r // 128, r % 128]
        second = slot_s[(r + 1) // 128, (r + 1) % 128]
        send[pl.ds(first, SENT), :] = both[:4, :CELLS]
        send[pl.ds(second, SENT), :] = both[4:, CELLS:]

    for copy, (start, size) in zip(chunk_copies, spans(CONTRIB_SIZES)):
        copy.wait()
        for r in range(start, start + size, 2):
            pair(r)


def contributions(row_owner, row_target, flux, remap):
    return pl.pallas_call(
        contrib_kernel,
        out_shape=(
            jax.ShapeDtypeStruct((DEV * BLOCK, CELLS), F32),
            jax.ShapeDtypeStruct((2, 128), jnp.int32),
            VMEM((NEAR, 128, 128), BF16),
        ),
        in_specs=[pl.BlockSpec(memory_space=pltpu.HBM)] * 4,
        out_specs=tuple(vmem_specs(3)),
        scratch_shapes=[
            VMEM((ROWS - NEAR, 128, 128), BF16),
            VMEM((6, ROWS, 128), F32),
            VMEM((ROWS * SENT, 128), F32),
            VMEM((2, 128), jnp.int32),
            VMEM((2, 128), jnp.int32),
            VMEM((2, 128), jnp.int32),
            SMEM((2, 128), jnp.int32),
            pltpu.SemaphoreType.DMA((len(CONTRIB_SIZES),)),
            pltpu.SemaphoreType.DMA((4,)),
        ],
        compiler_params=params(24),
        cost_estimate=pl.CostEstimate(flops=10**9, bytes_accessed=10_000_000, transcendentals=0),
        name="contrib",
    )(row_owner, row_target, flux, remap)


def edge_kernel(tracers, east_vel, north_vel, levels, to_east, to_west, to_north, to_south):
    lev = levels[...].astype(F32)
    lane = iota((CY, 128), 1)
    zero = jnp.zeros((CY, 128), F32)
    east, west = zero, zero
    planes = [tracers[p] for p in range(16)] + [lev] + [east_vel[k] for k in range(LEV)]
    for p, plane in enumerate(planes):
        east = jnp.where(lane == p, pltpu.roll(plane, (p + 1) % 128, 1), east)
        if p < 17:
            west = jnp.where(lane == p, plane if p == 0 else pltpu.roll(plane, p, 1), west)
    to_east[...] = east
    to_west[...] = west
    to_north[...] = zero
    to_south[...] = zero
    for p in range(16):
        to_north[p : p + 1, :] = tracers[p, CY - 1 : CY, :]
        to_south[p : p + 1, :] = tracers[p, 0:1, :]
    to_north[16:17, :] = lev[CY - 1 : CY]
    to_south[16:17, :] = lev[0:1]
    for k in range(LEV):
        to_north[17 + k : 18 + k, :] = north_vel[k, CY - 1 : CY, :]


def edges(tracers, east_vel, north_vel, levels):
    return pl.pallas_call(
        edge_kernel,
        out_shape=tuple(jax.ShapeDtypeStruct((CY, 128), F32) for _ in range(4)),
        in_specs=vmem_specs(4),
        out_specs=tuple(vmem_specs(4)),
        compiler_params=params(8),
        cost_estimate=pl.CostEstimate(flops=10**5, bytes_accessed=1_000_000, transcendentals=0),
        name="edges",
    )(tracers, east_vel, north_vel, levels)


def advect_kernel(tracers, east_vel, north_vel, levels, out):
    lane_last = iota((CY, 128), 1) == 127
    row_last = iota((CY, 128), 0) == CY - 1
    lev = levels[...].astype(F32)
    lev_e = jnp.where(lane_last, 0.0, pltpu.roll(lev, 127, 1))
    lev_n = jnp.where(row_last, 0.0, pltpu.roll(lev, CY - 1, 0))
    for k in range(LEV):
        depth = float(k)
        wet = (lev > depth).astype(F32)
        wet_e = wet * (lev_e > depth).astype(F32)
        wet_n = wet * (lev_n > depth).astype(F32)
        vel_e, vel_n = east_vel[k], north_vel[k]
        e_pos, e_neg = jnp.maximum(vel_e, 0.0), jnp.minimum(vel_e, 0.0)
        n_pos, n_neg = jnp.maximum(vel_n, 0.0), jnp.minimum(vel_n, 0.0)
        for t in range(2):
            p = t * LEV + k
            here = tracers[p]
            flux_e = (e_pos * here + e_neg * pltpu.roll(here, 127, 1)) * wet_e
            flux_n = (n_pos * here + n_neg * pltpu.roll(here, CY - 1, 0)) * wet_n
            out[p] = here - (flux_e - pltpu.roll(flux_e, 1, 1)) - (flux_n - pltpu.roll(flux_n, 1, 0))


def advected(*args):
    return pl.pallas_call(
        advect_kernel,
        out_shape=jax.ShapeDtypeStruct((16, CY, 128), F32),
        in_specs=vmem_specs(4),
        out_specs=pl.BlockSpec(memory_space=VMEM),
        compiler_params=params(8),
        cost_estimate=pl.CostEstimate(flops=10**6, bytes_accessed=2_000_000, transcendentals=0),
        name="advect",
    )(*args)


def face(vel, low, high, lev_low, lev_high, depth):
    wet = (lev_low > depth).astype(F32) * (lev_high > depth).astype(F32)
    return (jnp.maximum(vel, 0.0) * low + jnp.minimum(vel, 0.0) * high) * wet


def side_face(low, high):
    lane = iota((CY, 128), 1)
    packed = low[...]
    vel = jnp.where(lane < LEV, pltpu.roll(packed, 128 - 17, 1), pltpu.roll(packed, 128 - 9, 1))
    return face(
        vel, packed, high[...], low[:, 16:17], high[:, 16:17], (lane % LEV).astype(F32)
    )


def end_face(low, high):
    vel = jnp.concatenate([low[17 : 17 + LEV, :]] * 2, axis=0)
    depth = (iota((2 * LEV, 128), 0) % LEV).astype(F32)
    return face(
        vel, low[0 : 2 * LEV, :], high[0 : 2 * LEV, :], low[16:17, :], high[16:17, :], depth
    )


def ocean_kernel(
    got,
    inner,
    kappa,
    levels,
    to_east,
    to_west,
    to_north,
    to_south,
    west_in,
    east_in,
    south_in,
    north_in,
    turned_hbm,
    after_hbm,
    answer,
    after,
    sem,
):
    lane, row = iota((CY, 128), 1), iota((CY, 128), 0)
    from_west, to_next = side_face(west_in, to_west), side_face(to_east, east_in)
    from_south, to_top = end_face(south_in, to_south), end_face(to_north, north_in)
    carried = []
    for p in range(2 * LEV):
        west = from_west if p == 0 else pltpu.roll(from_west, 128 - p, 1)
        sides = jnp.where(lane == 0, west, 0.0)
        sides = jnp.where(lane == 127, -pltpu.roll(to_next, 127 - p, 1), sides)
        ends = jnp.where(row == 0, from_south[p : p + 1, :], 0.0)
        ends = jnp.where(row == CY - 1, -to_top[p : p + 1, :], ends)
        carried.append(inner[p] + sides + ends)
    tags = jnp.transpose(got[pl.ds(CAP * SENT, DEV, stride=BLOCK), :])
    labels = iota((CY, DEV), 0).astype(F32) + 1.0
    select = jnp.concatenate(
        [(tags[s : s + 1, :] == labels).astype(F32) for s in range(CAP)], axis=1
    ).astype(BF16)
    forcing = []
    for f in range(SENT):
        rows = jnp.concatenate(
            [got[pl.ds(s * SENT + f, DEV, stride=BLOCK), :] for s in range(CAP)], axis=0
        )
        high, low = split(rows)
        both = jnp.dot(select, jnp.concatenate([high, low], axis=1), preferred_element_type=F32)
        forcing.append(both[:, :CELLS] + both[:, CELLS:])
    short, surface_heat, fresh, wind = forcing
    lev = levels[...]
    stirring = 0.25 * wind * wind
    wet = [(lev > k).astype(F32) for k in range(LEV)]
    link = [None] + [
        (kappa[k] + stirring * math.exp(-0.5 * k)) * wet[k] for k in range(1, LEV)
    ]
    gains, offsets = [], []
    for k in range(LEV):
        fraction = math.exp(-0.5 * k) - math.exp(-0.5 * (k + 1))
        heat = wet[k] * (fraction * short)
        warmth, salt = carried[k] + heat, carried[LEV + k]
        if k == 0:
            warmth = warmth + 0.5 * wet[0] * surface_heat
            salt = salt + 0.5 * wet[0] * fresh
        diagonal = 1.0 if k == 0 else 1.0 + link[k]
        if k < LEV - 1:
            diagonal = diagonal + link[k + 1]
        if k > 0:
            diagonal = diagonal - link[k] * gains[-1]
            warmth = warmth + link[k] * offsets[-1][0]
            salt = salt + link[k] * offsets[-1][1]
        inverse = 1.0 / diagonal
        if k < LEV - 1:
            gains.append(link[k + 1] * inverse)
        offsets.append((warmth * inverse, salt * inverse))
    warmth, salt = offsets[-1]
    after[LEV - 1], after[2 * LEV - 1] = warmth, salt
    for k in range(LEV - 2, -1, -1):
        warmth = offsets[k][0] + gains[k] * warmth
        salt = offsets[k][1] + gains[k] * salt
        after[k], after[LEV + k] = warmth, salt
    after_copy = pltpu.make_async_copy(after, after_hbm, sem)
    after_copy.start()
    high, low = split(jnp.concatenate([warmth, salt], axis=1))
    picked = lax.dot_general(
        select,
        jnp.concatenate([high, low], axis=1),
        (((0,), (0,)), ((), ())),
        preferred_element_type=F32,
    )
    for s in range(CAP):
        for f in range(2):
            rows = picked[s * DEV : (s + 1) * DEV]
            answer[:, 2 * s + f, :] = (
                rows[:, f * CELLS : (f + 1) * CELLS] + rows[:, (2 + f) * CELLS : (3 + f) * CELLS]
            )
    after_copy.wait()


def ocean(*args):
    return pl.pallas_call(
        ocean_kernel,
        out_shape=(
            pltpu.HBM((16, CY, 128), F32),
            jax.ShapeDtypeStruct((DEV, 2 * CAP, CELLS), F32),
        ),
        in_specs=vmem_specs(12) + [pl.BlockSpec(memory_space=pltpu.HBM)],
        out_specs=(pl.BlockSpec(memory_space=pltpu.HBM), pl.BlockSpec(memory_space=VMEM)),
        scratch_shapes=[VMEM((16, CY, 128), F32), pltpu.SemaphoreType.DMA],
        compiler_params=params(24),
        cost_estimate=pl.CostEstimate(flops=10**8, bytes_accessed=4_000_000, transcendentals=0),
        name="ocean",
    )(*args)


def turn_kernel(inner, remap_hbm, turned_hbm, mid, blocks, turned, mid_blocks, in_sems, out_sems):
    parts = [pl.ds(i * PIECE, PIECE) for i in range(TURNED // PIECE)]
    reads = [
        pltpu.make_async_copy(
            remap_hbm.at[pl.ds(ROWS - TURNED + i * PIECE, PIECE)], blocks.at[part], in_sems.at[i]
        )
        for i, part in enumerate(parts)
    ]
    writes = [
        pltpu.make_async_copy(turned.at[part], turned_hbm.at[part], out_sems.at[i])
        for i, part in enumerate(parts)
    ]
    mid_read = pltpu.make_async_copy(
        remap_hbm.at[pl.ds(NEAR, MID)], mid_blocks, in_sems.at[TURNED // PIECE]
    )
    for read in reads:
        read.start()
    mid_read.start()
    for i, (read, write) in enumerate(zip(reads, writes)):
        read.wait()
        for r in range(i * PIECE, (i + 1) * PIECE):
            turned[r] = blocks[r].T
        write.start()
    mid_read.wait()
    for r in range(MID):
        mid[r] = mid_blocks[r].T
    for write in writes:
        write.wait()


def turn(inner, remap):
    return pl.pallas_call(
        turn_kernel,
        out_shape=(pltpu.HBM((TURNED, 128, 128), BF16), VMEM((MID, 128, 128), BF16)),
        in_specs=vmem_specs(1) + [pl.BlockSpec(memory_space=pltpu.HBM)],
        out_specs=(pl.BlockSpec(memory_space=pltpu.HBM), pl.BlockSpec(memory_space=VMEM)),
        scratch_shapes=[
            VMEM((TURNED, 128, 128), BF16),
            VMEM((TURNED, 128, 128), BF16),
            VMEM((MID, 128, 128), BF16),
            pltpu.SemaphoreType.DMA((TURNED // PIECE + 1,)),
            pltpu.SemaphoreType.DMA((TURNED // PIECE,)),
        ],
        compiler_params=params(16),
        cost_estimate=pl.CostEstimate(flops=10**6, bytes_accessed=6_000_000, transcendentals=0),
        name="turn",
    )(inner, remap)


def state_kernel(slots_in, returned, near, mid, remap_hbm, turned_hbm, out_hbm, far, turned, rows, out, slots, sems, out_sems, sem):
    far_copies = block_copies(remap_hbm, near, far, sems, FAR_SIZES, NEAR + MID)
    slot_copy = pltpu.make_async_copy(slots_in, slots, sem)
    slot_copy.start()
    turned_copy = pltpu.make_async_copy(turned_hbm, turned, sems.at[len(FAR_SIZES)])
    for copy in far_copies:
        copy.start()
    turned_copy.start()
    slot_copy.wait()
    for r in range(ROWS):
        rows[2 * r : 2 * r + 2, :] = returned[pl.ds(slots[r // 128, r % 128], 2), :]

    def four_rows(r, blocks, transposed=False):
        high, low = split(rows[2 * r : 2 * r + 8, :])
        left = jnp.concatenate([high, low], axis=0)
        if transposed:
            right = jnp.concatenate([blocks[j] for j in range(4)], axis=1)
            four = jnp.dot(left, right, preferred_element_type=F32)
        else:
            four = lax.dot_general(
                left,
                blocks.reshape(4 * 128, 128),
                (((1,), (1,)), ((), ())),
                preferred_element_type=F32,
            )
        four = four[:8] + four[8:]
        for j in range(4):
            out[r + j] = four[2 * j : 2 * j + 2, j * 128 : (j + 1) * 128]

    out_copies = []

    def hand_on(start, size):
        part = pl.ds(start, size)
        copy = pltpu.make_async_copy(out.at[part], out_hbm.at[part], out_sems.at[len(out_copies)])
        copy.start()
        out_copies.append(copy)

    for r in range(0, NEAR, 4):
        four_rows(r, near[r : r + 4])
    for r in range(0, MID, 4):
        four_rows(NEAR + r, mid[r : r + 4], True)
    hand_on(0, NEAR + MID)
    for copy, (start, size) in zip(far_copies, spans(FAR_SIZES)):
        copy.wait()
        for r in range(MID + start, MID + start + size, 4):
            four_rows(NEAR + r, far[r : r + 4])
        hand_on(NEAR + MID + start, size)
    turned_copy.wait()
    for r in range(0, TURNED, 4):
        four_rows(ROWS - TURNED + r, turned[r : r + 4], True)
    hand_on(ROWS - TURNED, TURNED)
    for copy in out_copies:
        copy.wait()


def state(slots, returned, near, mid, remap, turned):
    return pl.pallas_call(
        state_kernel,
        out_shape=pltpu.HBM((ROWS, 2, 128), F32),
        in_specs=vmem_specs(4) + [pl.BlockSpec(memory_space=pltpu.HBM)] * 2,
        out_specs=pl.BlockSpec(memory_space=pltpu.HBM),
        scratch_shapes=[
            VMEM((ROWS - NEAR - TURNED, 128, 128), BF16),
            VMEM((TURNED, 128, 128), BF16),
            VMEM((2 * ROWS, 128), F32),
            VMEM((ROWS, 2, 128), F32),
            SMEM((2, 128), jnp.int32),
            pltpu.SemaphoreType.DMA((len(FAR_SIZES) + 1,)),
            pltpu.SemaphoreType.DMA((len(FAR_SIZES) + 2,)),
            pltpu.SemaphoreType.DMA,
        ],
        compiler_params=params(20),
        cost_estimate=pl.CostEstimate(flops=10**9, bytes_accessed=9_000_000, transcendentals=0),
        name="state",
    )(slots, returned, near, mid, remap, turned)


def shifts(count, wraps):
    up = [(i, i + 1) for i in range(count - 1)] + ([(count - 1, 0)] if wraps else [])
    return up, [(b, a) for a, b in up]


def on_device(
    atmos_flux, remap_blocks, row_owner, row_target, tracers, east_vel, north_vel, mix_kappa, levels
):
    axes = ("lon", "lat")
    planes = tracers.reshape(2 * LEV, CY, CELLS)
    to_east, to_west, to_north, to_south = edges(planes, east_vel, north_vel, levels)
    eastward, westward = shifts(lax.axis_size("lon"), True)
    northward, southward = shifts(lax.axis_size("lat"), False)
    west_in = lax.ppermute(to_east, "lon", eastward)
    east_in = lax.ppermute(to_west, "lon", westward)
    south_in = lax.ppermute(to_north, "lat", northward)
    north_in = lax.ppermute(to_south, "lat", southward)
    send, slots, near = contributions(
        in_hbm(row_owner.reshape(2, 128)),
        in_hbm(row_target.reshape(2, 128)),
        in_hbm(jnp.transpose(atmos_flux, (1, 0, 2))),
        in_hbm(remap_blocks),
    )
    got = lax.all_to_all(
        send.reshape(DEV, BLOCK, 1, CELLS), axes, split_axis=0, concat_axis=0, tiled=True
    )
    inner = advected(planes, east_vel, north_vel, levels)
    turned, mid = turn(inner, in_hbm(remap_blocks))
    after, answer = ocean(
        got.reshape(DEV * BLOCK, CELLS),
        inner,
        mix_kappa,
        levels,
        to_east,
        to_west,
        to_north,
        to_south,
        west_in,
        east_in,
        south_in,
        north_in,
        in_hbm(turned),
    )
    returned = lax.all_to_all(answer, axes, split_axis=0, concat_axis=0, tiled=True)
    atmos_state = state(
        slots,
        returned.reshape(DEV * 2 * CAP, CELLS),
        pltpu.with_memory_space_constraint(near, VMEM),
        pltpu.with_memory_space_constraint(mid, VMEM),
        in_hbm(remap_blocks),
        in_hbm(turned),
    )
    return after.reshape(2, LEV, CY, CELLS), atmos_state


def solution(mesh):
    row = ("lon", "lat")
    in_specs = (
        P(row, None, None),
        P(row, None, None),
        P(row, None),
        P(row),
        P(None, None, "lat", "lon"),
        P(None, "lat", "lon"),
        P(None, "lat", "lon"),
        P(None, "lat", "lon"),
        P("lat", "lon"),
    )
    out_specs = (P(None, None, "lat", "lon"), P(row, None, None))
    return jax.shard_map(
        on_device, mesh=mesh, in_specs=in_specs, out_specs=out_specs, check_vma=False
    )
```
